32 devices in a mesh: dp: 16 (over z, y, x), space: 2 (over core).
Axes of the slice: x: 2, y: 2, z: 4, core: 2. Of those that a mesh axis runs over, the one named last changes fastest.
Arguments:
- activations: bfloat16 [16, 32, 8, 256], P('dp', None, 'space'), may hold values from -6 to 6
- cotangent: bfloat16 [16, 128, 4, 64], P('dp', None, 'space'), may hold values from -12 to 12
- weight_mid: bfloat16 [3, 3, 3, 32, 64], replicated, may hold values from -0.21875 to 0.21875
- weight_deep: bfloat16 [3, 3, 3, 64, 128], replicated, may hold values from -0.15625 to 0.15625
Outputs:
- grad_input: bfloat16 [16, 32, 8, 256], P('dp', None, 'space')
- grad_mid: float32 [3, 3, 3, 32, 64], replicated
- grad_deep: float32 [3, 3, 3, 64, 128], replicated
The draws below stay inside these ranges and needn't reach their ends.
All inputs are finite; a program needn't handle non-finite values.
Results may differ from the reference program's by a relative error of at most 0.0059.
Values may be sent and summed in bfloat16 or wider, within the bound.
A program may use at most 64 MiB of HBM per device.

```python
from functools import partial
import jax
import jax.numpy as jnp
from jax import lax

C1 = 32
C2 = 64
C3 = 128
ROWS = 4
COLS = 64
SAMPLES = 16
DEPTH = 8
PLANE = 256
PLANE3 = 64
DEPTH3 = 4


def shard_levels(own_key, shape, cuts, smallest, high):
    def one(axis_at, shards_of):
        draws = jax.random.uniform(jax.random.fold_in(jax.random.fold_in(own_key, 6), axis_at), (shards_of,), jnp.float32, smallest / len(cuts), high / len(cuts))
        return jnp.repeat(jnp.exp(draws), shape[axis_at] // shards_of).reshape((-1,) + (1,) * (len(shape) - axis_at - 1))

    gain = one(*cuts[0])
    for cut in cuts[1:]:
        gain = gain * one(*cut)
    return gain


def scatter_about(stream_key, shape, scale, reach, split=(), dtype=jnp.bfloat16):
    loudness = shard_levels(stream_key, shape, split, -0.22, 0.18) if split else 1.0
    values = jax.random.normal(stream_key, shape, jnp.float32) * scale * loudness
    return jnp.minimum(jnp.maximum(values, -reach), reach).astype(dtype)


def setup_inputs(seed: int = 0) -> dict:
    keys = jax.random.split(jax.random.key(seed), 5)
    activations = scatter_about(keys[0], (SAMPLES, C1, DEPTH, PLANE), 1.0, 6.0, ((0, 16), (2, 2)))
    cotangent = scatter_about(keys[1], (SAMPLES, C3, DEPTH3, PLANE3), 2.0, 12.0, ((0, 16), (2, 2)))
    weight_mid = scatter_about(keys[2], (3, 3, 3, C1, C2), (27 * C1) ** -0.5, 0.21875)
    weight_deep = scatter_about(keys[3], (3, 3, 3, C2, C3), (27 * C2) ** -0.5, 0.15625)
    return dict(activations=activations, cotangent=cotangent, weight_mid=weight_mid, weight_deep=weight_deep)


def conv_same(field, kernel):
    return lax.conv_general_dilated(field[None], kernel, (1, 1, 1), 'SAME', dimension_numbers=('NCDHW', 'DHWIO', 'NCDHW'), precision=lax.Precision.HIGHEST)[0]

def flip_taps(kernel):
    return jnp.transpose(kernel[::-1, ::-1, ::-1], (0, 1, 2, 4, 3))

def pool_cube(values):
    chans, depth_len, row_count, col_count = values.shape
    blocks = values.reshape(chans, depth_len // 2, 2, row_count // 2, 2, col_count // 2, 2)
    return lax.optimization_barrier(jnp.mean(blocks, axis=(2, 4, 6)))

def upsample_cube(values):
    spread = jnp.repeat(values, 2, axis=1)
    spread = jnp.repeat(spread, 2, axis=2)
    return jnp.repeat(spread, 2, axis=3)

def gelu_back(pre_values, upstream):
    return jax.vjp(partial(jax.nn.gelu, approximate=True), pre_values)[1](upstream)[0]

def weight_terms(field, grad_out, kernel):
    return jax.vjp(lambda kern: conv_same(field, kern), kernel)[1](grad_out)[0]

def one_sample(source, upstream, mid_kernel, deep_kernel):
    depth_len = source.shape[1]
    source_f = source.astype(jnp.float32).reshape(C1, depth_len, ROWS, COLS)
    pre_mid = conv_same(source_f, mid_kernel)
    pooled = pool_cube(jax.nn.gelu(pre_mid, approximate=True)).astype(jnp.bfloat16)
    pooled_f = lax.optimization_barrier(pooled).astype(jnp.float32)
    pre_deep = conv_same(pooled_f, deep_kernel)
    upstream_f = upstream.astype(jnp.float32).reshape(C3, depth_len // 2, ROWS // 2, COLS // 2)
    deep_grad = gelu_back(pre_deep, upstream_f).astype(jnp.bfloat16)
    deep_grad_f = lax.optimization_barrier(deep_grad).astype(jnp.float32)
    terms_deep = weight_terms(pooled_f, deep_grad_f, deep_kernel)
    back_pooled = conv_same(deep_grad_f, flip_taps(deep_kernel))
    spread = upsample_cube(back_pooled) * 0.125
    mid_grad = gelu_back(pre_mid, spread).astype(jnp.bfloat16)
    mid_grad_f = lax.optimization_barrier(mid_grad).astype(jnp.float32)
    terms_mid = weight_terms(source_f, mid_grad_f, mid_kernel)
    grad_in = conv_same(mid_grad_f, flip_taps(mid_kernel)).astype(jnp.bfloat16)
    return (grad_in.reshape(C1, depth_len, ROWS * COLS), terms_mid, terms_deep)

def reference(activations, cotangent, weight_mid, weight_deep):
    mid_kernel = weight_mid.astype(jnp.float32)
    deep_kernel = weight_deep.astype(jnp.float32)

    def advance(carry, inputs):
        grad_in, terms_mid, terms_deep = one_sample(inputs[0], inputs[1], mid_kernel, deep_kernel)
        return ((carry[0] + terms_mid, carry[1] + terms_deep), grad_in)
    start = (jnp.zeros(weight_mid.shape, jnp.float32), jnp.zeros(weight_deep.shape, jnp.float32))
    totals, grad_input = lax.scan(advance, start, (activations, cotangent))
    return (grad_input, totals[0] / SAMPLES, totals[1] / SAMPLES)
```

```python
import functools

import jax
import jax.numpy as jnp
from jax import lax
from jax.experimental import pallas as pl
from jax.experimental.pallas import tpu as pltpu
from jax.sharding import PartitionSpec as P

ROWS = 4
COLS = 64
LANES = 128
ROW_TILE = 16


def group_stages(samples, slabs):
    stages = [("space", slabs, 1)]
    stride = 1
    for size in (2, 2, 4):
        if samples // stride % size == 0:
            stages.append(("dp", size, stride))
            stride *= size
    if samples // stride > 1:
        stages.append(("dp", samples // stride, stride))
    return stages


def place(axis, size, stride):
    return lax.rem(lax.axis_index(axis) // stride, size)


def partner(axis, size, stride, step):
    own = place(axis, size, stride)
    other = lax.rem(own + step, size)
    dp, space = lax.axis_index("dp"), lax.axis_index("space")
    if axis == "space":
        return other, (dp, other)
    return other, (dp + (other - own) * stride, space)


def rows_at(start, count):
    return pl.ds(pl.multiple_of(start, ROW_TILE), count)


class Reduction:
    def __init__(self, stages, total, outgoing, gathered, landing, sems):
        self.stages, self.total, self.outgoing = stages, total, outgoing
        self.gathered, self.landing, self.sems = gathered, landing, sems
        self.start, self.length = 0, total.shape[0]
        self.starts, self.copies, self.sent, self.used = [], [], [], 0

    def copy(self, source, target, device):
        send, recv = self.sems
        made = pltpu.make_async_remote_copy(
            src_ref=source,
            dst_ref=target,
            send_sem=send.at[self.used],
            recv_sem=recv.at[self.used],
            device_id=device,
            device_id_type=pl.DeviceIdType.MESH,
        )
        self.used += 1
        made.start()
        self.copies.append(made)

    def scatter_start(self, index):
        axis, size, stride = self.stages[index]
        piece = self.length // size
        for step in range(1, size):
            other, device = partner(axis, size, stride, step)
            window = rows_at(self.start + other * piece, piece)
            self.outgoing[window] = self.total[window].astype(jnp.bfloat16)
            self.copy(self.outgoing.at[window], self.landing[index].at[step - 1], device)
        self.starts.append(self.start)
        self.start = self.start + place(axis, size, stride) * piece
        self.length = piece

    def scatter_finish(self, index):
        window = rows_at(self.start, self.length)
        value = self.total[window]
        for step, made in enumerate(self.copies):
            made.wait_recv()
            value = value + self.landing[index][step].astype(jnp.float32)
        self.total[window] = value
        self.sent += self.copies
        self.copies = []

    def gather_own(self):
        window = rows_at(self.start, self.length)
        self.gathered[window] = self.total[window].astype(jnp.bfloat16)

    def gather_start(self, index):
        axis, size, stride = self.stages[index]
        window = rows_at(self.start, self.length)
        for step in range(1, size):
            _, device = partner(axis, size, stride, step)
            self.copy(self.gathered.at[window], self.gathered.at[window], device)
        self.start = self.starts[index]
        self.length = self.length * size

    def gather_finish(self):
        for made in self.copies:
            made.wait_recv()
        self.sent += self.copies
        self.copies = []

    def drain(self):
        for made in self.sent:
            made.wait_send()


def reduction_rows(rows, devices):
    return -(-rows // (devices * ROW_TILE)) * ROW_TILE * devices


def reduction_scratch(stages, rows):
    shapes = [
        pltpu.VMEM((rows, LANES), jnp.float32),
        pltpu.VMEM((rows, LANES), jnp.bfloat16),
        pltpu.VMEM((rows, LANES), jnp.bfloat16),
    ]
    length, count = rows, 0
    for _, size, _ in stages:
        length //= size
        count += 2 * (size - 1)
        shapes.append(pltpu.VMEM((size - 1, length, LANES), jnp.bfloat16))
    return shapes + [pltpu.SemaphoreType.DMA((count,)), pltpu.SemaphoreType.DMA((count,))]


def greet(stages):
    barrier = pltpu.get_barrier_semaphore()
    count = 0
    for axis, size, stride in stages:
        for step in range(1, size):
            _, device = partner(axis, size, stride, step)
            pl.semaphore_signal(barrier, inc=1, device_id=device, device_id_type=pl.DeviceIdType.MESH)
            count += 1
    pl.semaphore_wait(barrier, count)


def sum_kernel(stages, scale, mid_ref, deep_ref, mid_out, deep_out, total, outgoing, gathered, *rest):
    half = mid_ref.shape[0] // 2
    wide = mid_ref.shape[1]
    deep_rows = deep_ref.shape[0]
    used = deep_rows + half
    total[:deep_rows] = deep_ref[...]
    total[deep_rows:used, :wide] = mid_ref[:half]
    total[deep_rows:used, wide:] = mid_ref[half:]
    if used < total.shape[0]:
        total[used:] = jnp.zeros((total.shape[0] - used, LANES), jnp.float32)
    greet(stages)
    work = Reduction(stages, total, outgoing, gathered, rest[: len(stages)], rest[len(stages) :])
    for index in range(len(stages)):
        work.scatter_start(index)
        work.scatter_finish(index)
    work.gather_own()
    for index in reversed(range(len(stages))):
        work.gather_start(index)
        work.gather_finish()
    deep_out[...] = gathered[:deep_rows].astype(jnp.float32) * scale
    packed = gathered[deep_rows:used].astype(jnp.float32) * scale
    mid_out[:half] = packed[:, :wide]
    mid_out[half:] = packed[:, wide:]
    work.drain()


def summed_terms(mid_terms, deep_terms):
    samples, slabs = lax.axis_size("dp"), lax.axis_size("space")
    stages = group_stages(samples, slabs)
    mid_flat = mid_terms.reshape(-1, mid_terms.shape[-1])
    deep_flat = deep_terms.reshape(-1, LANES)
    rows = reduction_rows(deep_flat.shape[0] + mid_flat.shape[0] // 2, samples * slabs)
    mid_sum, deep_sum = pl.pallas_call(
        functools.partial(sum_kernel, stages, 1.0 / samples),
        out_shape=[
            jax.ShapeDtypeStruct(mid_flat.shape, jnp.float32),
            jax.ShapeDtypeStruct(deep_flat.shape, jnp.float32),
        ],
        in_specs=[pl.BlockSpec(memory_space=pltpu.VMEM)] * 2,
        out_specs=[pl.BlockSpec(memory_space=pltpu.VMEM)] * 2,
        scratch_shapes=reduction_scratch(stages, rows),
        compiler_params=pltpu.CompilerParams(
            collective_id=0, has_side_effects=True, vmem_limit_bytes=48 * 1024 * 1024
        ),
    )(mid_flat, deep_flat)
    return mid_sum.reshape(mid_terms.shape), deep_sum.reshape(deep_terms.shape)

def extended(block, sides, width):
    for axis, dim in sides:
        count = lax.axis_size(axis)
        forward = [(i, i + 1) for i in range(count - 1)]
        backward = [(target, source) for source, target in forward]
        low = lax.ppermute(
            lax.slice_in_dim(block, block.shape[dim] - width, None, axis=dim), axis, forward
        )
        high = lax.ppermute(lax.slice_in_dim(block, 0, width, axis=dim), axis, backward)
        block = jnp.concatenate([low, block, high], axis=dim)
    return block


def shifted(planes, row_step, col_step, row_count, col_count):
    margin = col_count + 1
    widened = jnp.pad(planes, ((0, 0), (0, 0), (margin, margin)))
    offset = margin + row_step * col_count + col_step
    moved_cells = widened[:, :, offset : offset + row_count * col_count]
    column = jnp.arange(row_count * col_count) % col_count + col_step
    inside = (column >= 0) & (column < col_count)
    return jnp.where(inside, moved_cells, jnp.zeros_like(moved_cells))


def tap_patches(padded, depth_tap, row_tap, row_count, col_count):
    depth_len = padded.shape[1] - 2
    planes = padded[:, depth_tap : depth_tap + depth_len]
    stacked = jnp.stack(
        [shifted(planes, row_tap - 1, col_tap - 1, row_count, col_count) for col_tap in range(3)]
    )
    return stacked.reshape(3 * planes.shape[0], depth_len * planes.shape[2])


def conv_cube(padded, kernel, row_count, col_count):
    depth_len = padded.shape[1] - 2
    chans_in = kernel.shape[3]
    chans_out = kernel.shape[4]
    summed = jnp.zeros((chans_out, depth_len * padded.shape[2]), jnp.float32)
    for depth_tap in range(3):
        for row_tap in range(3):
            patches = tap_patches(padded, depth_tap, row_tap, row_count, col_count)
            tap_block = kernel[depth_tap, row_tap].reshape(3 * chans_in, chans_out)
            summed = summed + lax.dot_general(
                tap_block, patches, (((0,), (0,)), ((), ())), preferred_element_type=jnp.float32
            )
    return summed.reshape(chans_out, depth_len, padded.shape[2])


def weight_terms(padded, grad_out, row_count, col_count):
    chans_in = padded.shape[0]
    chans_out = grad_out.shape[0]
    flat_grad = grad_out.reshape(chans_out, -1)
    pieces = []
    for depth_tap in range(3):
        for row_tap in range(3):
            patches = tap_patches(padded, depth_tap, row_tap, row_count, col_count)
            pieces.append(
                lax.dot_general(
                    patches, flat_grad, (((1,), (1,)), ((), ())), preferred_element_type=jnp.float32
                )
            )
    return jnp.stack(pieces).reshape(3, 3, 3, chans_in, chans_out)


def flip_taps(kernel):
    return jnp.transpose(kernel[::-1, ::-1, ::-1], (0, 1, 2, 4, 3))


def pool_matrix(row_count, col_count):
    cells = jnp.arange(row_count * col_count)
    target = cells // col_count // 2 * (col_count // 2) + cells % col_count // 2
    return (target[:, None] == jnp.arange(row_count * col_count // 4)[None, :]).astype(jnp.float32)


def pool_cube(values, matrix):
    chans, depth_len, plane_len = values.shape
    paired = values.reshape(chans, depth_len // 2, 2, plane_len).sum(axis=2)
    return jnp.einsum("cdp,pq->cdq", paired, matrix, precision=lax.Precision.HIGHEST) * 0.125


def upsample_cube(values, matrix):
    spread = jnp.einsum("cdq,pq->cdp", values, matrix, precision=lax.Precision.HIGHEST)
    return jnp.repeat(spread, 2, axis=1)


def gelu_fwd(values):
    return jax.nn.gelu(values, approximate=True)


def gelu_back(pre_values, upstream):
    return jax.vjp(gelu_fwd, pre_values)[1](upstream)[0]


def extend(field, width):
    return extended(field, (("space", 1),), width)


def shards(activations, cotangent, weight_mid, weight_deep):
    row_count = ROWS
    col_count = COLS
    source = activations[0]
    matrix = pool_matrix(row_count, col_count)
    widened = extend(source, 3)
    mid_pre_wide = conv_cube(widened, weight_mid, row_count, col_count)
    pooled_wide = pool_cube(gelu_fwd(mid_pre_wide), matrix)
    position = lax.axis_index("space")
    last_index = lax.axis_size("space") - 1
    depth_ids = jnp.arange(pooled_wide.shape[1])
    outside = (depth_ids == 0) & (position == 0) | (depth_ids == pooled_wide.shape[1] - 1) & (
        position == last_index
    )
    pooled_ext = jnp.where(outside[None, :, None], 0.0, pooled_wide).astype(jnp.bfloat16)
    mid_pre = mid_pre_wide[:, 2:-2]
    source_ext = widened[:, 2:-2]
    deep_pre = conv_cube(pooled_ext, weight_deep, row_count // 2, col_count // 2)
    deep_grad = gelu_back(deep_pre, cotangent[0].astype(jnp.float32)).astype(jnp.bfloat16)
    deep_terms = weight_terms(pooled_ext, deep_grad, row_count // 2, col_count // 2)
    back_pooled = conv_cube(
        extend(deep_grad, 1), flip_taps(weight_deep), row_count // 2, col_count // 2
    )
    spread = upsample_cube(back_pooled, matrix) * 0.125
    mid_grad = gelu_back(mid_pre, spread).astype(jnp.bfloat16)
    mid_terms = weight_terms(source_ext, mid_grad, row_count, col_count)
    grad_input = conv_cube(extend(mid_grad, 1), flip_taps(weight_mid), row_count, col_count).astype(
        jnp.bfloat16
    )
    grad_mid, grad_deep = summed_terms(mid_terms, deep_terms)
    return (grad_input[None], grad_mid, grad_deep)


def solution(mesh):
    in_specs = (P("dp", None, "space", None), P("dp", None, "space", None), P(), P())
    out_specs = (P("dp", None, "space", None), P(), P())
    return jax.shard_map(shards, mesh=mesh, in_specs=in_specs, out_specs=out_specs, check_vma=False)
```

```python
import functools

import jax
import jax.numpy as jnp
from jax import lax
from jax.experimental import pallas as pl
from jax.experimental.pallas import tpu as pltpu
from jax.sharding import PartitionSpec as P

ROWS = 4
COLS = 64
LANES = 128
ROW_TILE = 16


def group_stages(samples, slabs):
    stages = [("space", slabs, 1)]
    stride = 1
    for size in (2, 2, 4):
        if samples // stride % size == 0:
            stages.append(("dp", size, stride))
            stride *= size
    if samples // stride > 1:
        stages.append(("dp", samples // stride, stride))
    return stages


def place(axis, size, stride):
    return lax.rem(lax.axis_index(axis) // stride, size)


def partner(axis, size, stride, step):
    own = place(axis, size, stride)
    other = lax.rem(own + step, size)
    dp, space = lax.axis_index("dp"), lax.axis_index("space")
    if axis == "space":
        return other, (dp, other)
    return other, (dp + (other - own) * stride, space)


def rows_at(start, count):
    return pl.ds(pl.multiple_of(start, ROW_TILE), count)


class Reduction:
    def __init__(self, stages, total, outgoing, gathered, landing, sems):
        self.stages, self.total, self.outgoing = stages, total, outgoing
        self.gathered, self.landing, self.sems = gathered, landing, sems
        self.start, self.length = 0, total.shape[0]
        self.starts, self.copies, self.sent, self.used = [], [], [], 0

    def copy(self, source, target, device):
        send, recv = self.sems
        made = pltpu.make_async_remote_copy(
            src_ref=source,
            dst_ref=target,
            send_sem=send.at[self.used],
            recv_sem=recv.at[self.used],
            device_id=device,
            device_id_type=pl.DeviceIdType.MESH,
        )
        self.used += 1
        made.start()
        self.copies.append(made)

    def scatter_start(self, index):
        axis, size, stride = self.stages[index]
        piece = self.length // size
        for step in range(1, size):
            other, device = partner(axis, size, stride, step)
            window = rows_at(self.start + other * piece, piece)
            self.outgoing[window] = self.total[window].astype(jnp.bfloat16)
            self.copy(self.outgoing.at[window], self.landing[index].at[step - 1], device)
        self.starts.append(self.start)
        self.start = self.start + place(axis, size, stride) * piece
        self.length = piece

    def scatter_finish(self, index):
        window = rows_at(self.start, self.length)
        value = self.total[window]
        for step, made in enumerate(self.copies):
            made.wait_recv()
            value = value + self.landing[index][step].astype(jnp.float32)
        self.total[window] = value
        self.sent += self.copies
        self.copies = []

    def gather_own(self):
        window = rows_at(self.start, self.length)
        self.gathered[window] = self.total[window].astype(jnp.bfloat16)

    def gather_start(self, index):
        axis, size, stride = self.stages[index]
        window = rows_at(self.start, self.length)
        for step in range(1, size):
            _, device = partner(axis, size, stride, step)
            self.copy(self.gathered.at[window], self.gathered.at[window], device)
        self.start = self.starts[index]
        self.length = self.length * size

    def gather_finish(self):
        for made in self.copies:
            made.wait_recv()
        self.sent += self.copies
        self.copies = []

    def drain(self):
        for made in self.sent:
            made.wait_send()


def reduction_rows(rows, devices):
    return -(-rows // (devices * ROW_TILE)) * ROW_TILE * devices


def reduction_scratch(stages, rows):
    shapes = [
        pltpu.VMEM((rows, LANES), jnp.float32),
        pltpu.VMEM((rows, LANES), jnp.bfloat16),
        pltpu.VMEM((rows, LANES), jnp.bfloat16),
    ]
    length, count = rows, 0
    for _, size, _ in stages:
        length //= size
        count += 2 * (size - 1)
        shapes.append(pltpu.VMEM((size - 1, length, LANES), jnp.bfloat16))
    return shapes + [pltpu.SemaphoreType.DMA((count,)), pltpu.SemaphoreType.DMA((count,))]


def greet(stages):
    barrier = pltpu.get_barrier_semaphore()
    count = 0
    for axis, size, stride in stages:
        for step in range(1, size):
            _, device = partner(axis, size, stride, step)
            pl.semaphore_signal(barrier, inc=1, device_id=device, device_id_type=pl.DeviceIdType.MESH)
            count += 1
    pl.semaphore_wait(barrier, count)


def widened(edges, center, low, high):
    first = (edges[0].astype(jnp.float32) * low).astype(jnp.bfloat16)
    last = (edges[1].astype(jnp.float32) * high).astype(jnp.bfloat16)
    return jnp.concatenate([first, center, last], axis=1)


def fill_patches(patches, planes, row_count, col_count):
    chans, total = planes.shape
    cells = row_count * col_count
    span = total - 2 * cells
    lane = lax.broadcasted_iota(jnp.int32, (1, total), 1)
    col = lane % col_count
    row = lane // col_count % row_count
    for row_tap in range(3):
        for col_tap in range(3):
            row_at, col_at = row + (row_tap - 1), col + (col_tap - 1)
            inside = (row_at >= 0) & (row_at < row_count) & (col_at >= 0) & (col_at < col_count)
            offset = (row_tap - 1) * col_count + col_tap - 1
            moved = planes
            if offset:
                moved = pltpu.roll(planes, -offset % total, 1)
                moved = moved * jnp.where(inside, 1.0, 0.0).astype(jnp.bfloat16)
            for depth_tap in range(3):
                tap = (depth_tap * 3 + row_tap) * 3 + col_tap
                patches[tap * chans : (tap + 1) * chans] = moved[
                    :, depth_tap * cells : depth_tap * cells + span
                ]


def gelu_parts(values):
    scale = 0.7978845608028654
    square = values * values
    bend = jnp.tanh(scale * values * (1.0 + 0.044715 * square))
    half = 0.5 * (1.0 + bend)
    slope = half + 0.5 * values * (1.0 - bend * bend) * (scale * (1.0 + 0.134145 * square))
    return values * half, slope


def contract(left, right, left_dim, right_dim):
    return lax.dot_general(
        left, right, (((left_dim,), (right_dim,)), ((), ())), preferred_element_type=jnp.float32
    )


def pool_cells(values, row_count, col_count):
    cells = row_count * col_count
    pairs = [
        values[:, 2 * d * cells : (2 * d + 1) * cells] + values[:, (2 * d + 1) * cells : (2 * d + 2) * cells]
        for d in range(values.shape[1] // (2 * cells))
    ]
    paired = jnp.concatenate(pairs, axis=1)
    span = paired.shape[1]
    paired = paired + pltpu.roll(paired, span - 1, 1)
    paired = paired + pltpu.roll(paired, span - col_count, 1)
    small = cells // 4
    target = lax.broadcasted_iota(jnp.int32, (span, span // 4), 1)
    cell = target % small
    corner = (
        target // small * cells
        + cell // (col_count // 2) * (2 * col_count)
        + cell % (col_count // 2) * 2
    )
    here = lax.broadcasted_iota(jnp.int32, (span, span // 4), 0)
    picks = jnp.where(here == corner, 1.0, 0.0).astype(jnp.bfloat16)
    return contract((paired * 0.125).astype(jnp.bfloat16), picks, 1, 0).astype(jnp.bfloat16)


def spread_cells(values, row_count, col_count):
    cells = row_count * col_count
    chans, small_span = values.shape
    span = small_span * 8
    cell = lax.broadcasted_iota(jnp.int32, (small_span, span), 1)
    source = (
        cell // (2 * cells) * (cells // 4)
        + cell % cells // (2 * col_count) * (col_count // 2)
        + cell % col_count // 2
    )
    here = lax.broadcasted_iota(jnp.int32, (small_span, span), 0)
    copies = jnp.where(here == source, 1.0, 0.0).astype(jnp.bfloat16)
    high = values.astype(jnp.bfloat16)
    rest = values - high.astype(jnp.float32)
    middle = rest.astype(jnp.bfloat16)
    low = (rest - middle.astype(jnp.float32)).astype(jnp.bfloat16)
    wide = contract(jnp.concatenate([high, middle, low], axis=0), copies, 1, 0)
    return wide[:chans] + wide[chans : 2 * chans] + wide[2 * chans :]


def block_kernel(plans, layout, scale, *refs):
    refs = list(refs)

    def take(count):
        taken = refs[:count]
        del refs[:count]
        return taken

    source_ref, cot_ref, mid_ref, deep_ref = take(4)
    grad_in_ref, mid_out, deep_out = take(3)
    mid_patches, deep_patches, deep_back, mid_back, mid_flip, deep_flip = take(6)
    edges = [take(2) for _ in range(4)]
    edge_send, edge_recv = take(2)
    works = []
    for stages in plans:
        total, outgoing, gathered = take(3)
        landing = take(len(stages))
        works.append(Reduction(stages, total, outgoing, gathered, landing, take(2)))
    first, second, third = works
    row_count, col_count = layout
    cells = row_count * col_count
    small = cells // 4
    chans1 = source_ref.shape[0]
    chans2, chans3 = deep_ref.shape[0] // 27, deep_ref.shape[1]
    dp, space = lax.axis_index("dp"), lax.axis_index("space")
    slabs = lax.axis_size("space")
    low = jnp.where(space > 0, 1.0, 0.0)
    high = jnp.where(space < slabs - 1, 1.0, 0.0)

    def swap_start(index, planes, cells_here):
        leaving, arriving = edges[index]
        leaving[0] = planes[:, :cells_here]
        leaving[1] = planes[:, planes.shape[1] - cells_here :]
        made = []
        for side, other in ((0, lax.rem(space + slabs - 1, slabs)), (1, lax.rem(space + 1, slabs))):
            made.append(
                pltpu.make_async_remote_copy(
                    src_ref=leaving.at[side],
                    dst_ref=arriving.at[1 - side],
                    send_sem=edge_send.at[2 * index + side],
                    recv_sem=edge_recv.at[2 * index + side],
                    device_id=(dp, other),
                    device_id_type=pl.DeviceIdType.MESH,
                )
            )
            made[-1].start()
        return made

    def swap_finish(index, made, planes):
        for one in made:
            one.wait_recv()
        return widened(edges[index][1], planes, low, high)

    greet(plans[0])
    source = source_ref[...]
    swap0 = swap_start(0, source, cells)
    for tap in range(27):
        mid_flip[:, tap * chans2 : (tap + 1) * chans2] = mid_ref[(26 - tap) * chans1 : (27 - tap) * chans1]
        deep_flip[:, tap * chans3 : (tap + 1) * chans3] = deep_ref[(26 - tap) * chans2 : (27 - tap) * chans2]
    deep_rows = deep_ref.shape[0]
    cut = deep_rows // 2
    half = mid_out.shape[0] // 2
    for work, used in ((first, cut), (second, deep_rows - cut), (third, half)):
        spare = work.total.shape[0] - used
        if spare:
            work.total[used:] = jnp.zeros((spare, LANES), jnp.float32)
    fill_patches(mid_patches, swap_finish(0, swap0, source), row_count, col_count)
    mid_pre = contract(mid_ref[...], mid_patches[...], 0, 0)
    activated, mid_slope = gelu_parts(mid_pre)
    pooled = pool_cells(activated, row_count, col_count)
    swap1 = swap_start(1, pooled, small)
    fill_patches(deep_patches, swap_finish(1, swap1, pooled), row_count // 2, col_count // 2)
    deep_pre = contract(deep_ref[...], deep_patches[...], 0, 0)
    deep_grad = (cot_ref[...].astype(jnp.float32) * gelu_parts(deep_pre)[1]).astype(jnp.bfloat16)
    swap2 = swap_start(2, deep_grad, small)
    first.total[:cut] = contract(deep_patches[:cut], deep_grad, 1, 1)
    first.scatter_start(0)
    second.total[: deep_rows - cut] = contract(deep_patches[cut:], deep_grad, 1, 1)
    second.scatter_start(0)
    fill_patches(deep_back, swap_finish(2, swap2, deep_grad), row_count // 2, col_count // 2)
    back = contract(deep_flip[...], deep_back[...], 1, 0)
    upstream = spread_cells(back, row_count, col_count) * 0.125
    mid_grad = (upstream * mid_slope).astype(jnp.bfloat16)
    swap3 = swap_start(3, mid_grad, cells)
    depth = len(plans[0])

    def advance(work, index):
        work.scatter_finish(index)
        if index + 1 < depth:
            work.scatter_start(index + 1)
        else:
            work.gather_own()
            work.gather_start(depth - 1)

    def collect(work, index):
        work.gather_finish()
        if index:
            work.gather_start(index - 1)

    advance(first, 0)
    advance(second, 0)
    third.total[:half] = jnp.concatenate(
        [contract(mid_patches[:half], mid_grad, 1, 1), contract(mid_patches[half:], mid_grad, 1, 1)], axis=1
    )
    third.scatter_start(0)
    advance(first, 1)
    advance(second, 1)
    fill_patches(mid_back, swap_finish(3, swap3, mid_grad), row_count, col_count)
    advance(third, 0)
    grad_in_ref[...] = contract(mid_flip[...], mid_back[...], 1, 0).astype(jnp.bfloat16)
    for index in range(2, depth):
        advance(first, index)
        advance(second, index)
        advance(third, index - 1)
    collect(first, depth - 1)
    collect(second, depth - 1)
    advance(third, depth - 1)
    for index in reversed(range(depth - 1)):
        collect(first, index)
        collect(second, index)
        collect(third, index + 1)
    deep_out[:cut] = first.gathered[:cut].astype(jnp.float32) * scale
    deep_out[cut:] = second.gathered[: deep_rows - cut].astype(jnp.float32) * scale
    collect(third, 0)
    packed = third.gathered[:half].astype(jnp.float32) * scale
    mid_out[:half] = packed[:, : mid_out.shape[1]]
    mid_out[half:] = packed[:, mid_out.shape[1] :]
    for one in swap0 + swap1 + swap2 + swap3:
        one.wait_send()
    for work in works:
        work.drain()


def shards(activations, cotangent, weight_mid, weight_deep):
    samples, slabs = lax.axis_size("dp"), lax.axis_size("space")
    stages = group_stages(samples, slabs)
    swapped = [stages[0], stages[2], stages[1]] + stages[3:]
    plans = (stages, swapped, stages)
    chans1, chans2, chans3 = weight_mid.shape[3], weight_mid.shape[4], weight_deep.shape[4]
    source = activations[0].reshape(chans1, -1)
    upstream = cotangent[0].reshape(chans3, -1)
    mid_flat = weight_mid.reshape(-1, chans2)
    deep_flat = weight_deep.reshape(-1, chans3)
    cells, small = source.shape[1], upstream.shape[1]
    plane, small_plane = ROWS * COLS, ROWS * COLS // 4
    half_rows = reduction_rows(-(-deep_flat.shape[0] // 2), samples * slabs)
    mid_rows = reduction_rows(mid_flat.shape[0] // 2, samples * slabs)
    scratch = [
        pltpu.VMEM((27 * chans1, cells), jnp.bfloat16),
        pltpu.VMEM((27 * chans2, small), jnp.bfloat16),
        pltpu.VMEM((27 * chans3, small), jnp.bfloat16),
        pltpu.VMEM((27 * chans2, cells), jnp.bfloat16),
        pltpu.VMEM((chans1, 27 * chans2), jnp.bfloat16),
        pltpu.VMEM((chans2, 27 * chans3), jnp.bfloat16),
    ]
    for chans, width in ((chans1, plane), (chans2, small_plane), (chans3, small_plane), (chans2, plane)):
        scratch += [pltpu.VMEM((2, chans, width), jnp.bfloat16)] * 2
    scratch += [pltpu.SemaphoreType.DMA((8,)), pltpu.SemaphoreType.DMA((8,))]
    for plan, rows in zip(plans, (half_rows, half_rows, mid_rows)):
        scratch += reduction_scratch(plan, rows)
    grad_in, mid_sum, deep_sum = pl.pallas_call(
        functools.partial(block_kernel, plans, (ROWS, COLS), 1.0 / samples),
        out_shape=[
            jax.ShapeDtypeStruct(source.shape, jnp.bfloat16),
            jax.ShapeDtypeStruct(mid_flat.shape, jnp.float32),
            jax.ShapeDtypeStruct(deep_flat.shape, jnp.float32),
        ],
        in_specs=[pl.BlockSpec(memory_space=pltpu.VMEM)] * 4,
        out_specs=[pl.BlockSpec(memory_space=pltpu.VMEM)] * 3,
        scratch_shapes=scratch,
        compiler_params=pltpu.CompilerParams(
            collective_id=0, has_side_effects=True, vmem_limit_bytes=56 * 1024 * 1024
        ),
    )(source, upstream, mid_flat, deep_flat)
    return (
        grad_in.reshape(activations.shape),
        mid_sum.reshape(weight_mid.shape),
        deep_sum.reshape(weight_deep.shape),
    )


def solution(mesh):
    in_specs = (P("dp", None, "space", None), P("dp", None, "space", None), P(), P())
    out_specs = (P("dp", None, "space", None), P(), P())
    return jax.shard_map(shards, mesh=mesh, in_specs=in_specs, out_specs=out_specs, check_vma=False)
```

```python
import functools

import jax
import jax.numpy as jnp
from jax import lax
from jax.experimental import pallas as pl
from jax.experimental.pallas import tpu as pltpu
from jax.sharding import PartitionSpec as P

ROWS = 4
COLS = 64
LANES = 128
ROW_TILE = 16


def group_stages(samples, slabs):
    stages = [("space", slabs, 1)]
    stride = 1
    for size in (4, 4):
        if samples // stride % size == 0:
            stages.append(("dp", size, stride))
            stride *= size
    if samples // stride > 1:
        stages.append(("dp", samples // stride, stride))
    return stages


def place(axis, size, stride):
    return lax.rem(lax.axis_index(axis) // stride, size)


def partner(axis, size, stride, step):
    own = place(axis, size, stride)
    other = lax.rem(own + step, size)
    dp, space = lax.axis_index("dp"), lax.axis_index("space")
    if axis == "space":
        return other, (dp, other)
    return other, (dp + (other - own) * stride, space)


def rows_at(start, count):
    return pl.ds(pl.multiple_of(start, ROW_TILE), count)


class Reduction:
    def __init__(self, stages, total, outgoing, gathered, landing, sems):
        self.stages, self.total, self.outgoing = stages, total, outgoing
        self.gathered, self.landing, self.sems = gathered, landing, sems
        self.start, self.length = 0, total.shape[0]
        self.starts, self.copies, self.sent, self.used = [], [], [], 0

    def copy(self, source, target, device):
        send, recv = self.sems
        made = pltpu.make_async_remote_copy(
            src_ref=source,
            dst_ref=target,
            send_sem=send.at[self.used],
            recv_sem=recv.at[self.used],
            device_id=device,
            device_id_type=pl.DeviceIdType.MESH,
        )
        self.used += 1
        made.start()
        self.copies.append(made)

    def scatter_start(self, index):
        axis, size, stride = self.stages[index]
        piece = self.length // size
        for step in range(1, size):
            other, device = partner(axis, size, stride, step)
            window = rows_at(self.start + other * piece, piece)
            self.outgoing[window] = self.total[window].astype(jnp.bfloat16)
            self.copy(self.outgoing.at[window], self.landing[index].at[step - 1], device)
        self.starts.append(self.start)
        self.start = self.start + place(axis, size, stride) * piece
        self.length = piece

    def scatter_finish(self, index):
        window = rows_at(self.start, self.length)
        value = self.total[window]
        for step, made in enumerate(self.copies):
            made.wait_recv()
            value = value + self.landing[index][step].astype(jnp.float32)
        self.total[window] = value
        self.sent += self.copies
        self.copies = []

    def gather_own(self):
        window = rows_at(self.start, self.length)
        self.gathered[window] = self.total[window].astype(jnp.bfloat16)

    def gather_start(self, index):
        axis, size, stride = self.stages[index]
        window = rows_at(self.start, self.length)
        for step in range(1, size):
            _, device = partner(axis, size, stride, step)
            self.copy(self.gathered.at[window], self.gathered.at[window], device)
        self.start = self.starts[index]
        self.length = self.length * size

    def gather_finish(self):
        for made in self.copies:
            made.wait_recv()
        self.sent += self.copies
        self.copies = []

    def drain(self):
        for made in self.sent:
            made.wait_send()


def reduction_rows(rows, devices):
    return -(-rows // (devices * ROW_TILE)) * ROW_TILE * devices


def reduction_scratch(stages, rows):
    shapes = [
        pltpu.VMEM((rows, LANES), jnp.float32),
        pltpu.VMEM((rows, LANES), jnp.bfloat16),
        pltpu.VMEM((rows, LANES), jnp.bfloat16),
    ]
    length, count = rows, 0
    for _, size, _ in stages:
        length //= size
        count += 2 * (size - 1)
        shapes.append(pltpu.VMEM((size - 1, length, LANES), jnp.bfloat16))
    return shapes + [pltpu.SemaphoreType.DMA((count,)), pltpu.SemaphoreType.DMA((count,))]


def greet(stages):
    barrier = pltpu.get_barrier_semaphore()
    count = 0
    for axis, size, stride in stages:
        for step in range(1, size):
            _, device = partner(axis, size, stride, step)
            pl.semaphore_signal(barrier, inc=1, device_id=device, device_id_type=pl.DeviceIdType.MESH)
            count += 1
    pl.semaphore_wait(barrier, count)


def moved_planes(planes, row_tap, col_tap, row_count, col_count):
    offset = (row_tap - 1) * col_count + col_tap - 1
    if not offset:
        return planes
    total = planes.shape[1]
    lane = lax.broadcasted_iota(jnp.int32, (1, total), 1)
    col_at = lane % col_count + (col_tap - 1)
    row_at = lane // col_count % row_count + (row_tap - 1)
    inside = (row_at >= 0) & (row_at < row_count) & (col_at >= 0) & (col_at < col_count)
    keep = jnp.where(inside, 1.0, 0.0).astype(jnp.bfloat16)
    return pltpu.roll(planes, -offset % total, 1) * keep


def plane_taps():
    return [(row_tap, col_tap) for row_tap in range(3) for col_tap in range(3)]


def tap_rows(depth_tap, row_tap, col_tap, chans):
    tap = (depth_tap * 3 + row_tap) * 3 + col_tap
    return slice(tap * chans, (tap + 1) * chans)


def fill_inner(patches, planes, row_count, col_count):
    chans, span = planes.shape
    cells = row_count * col_count
    for taps in plane_taps():
        moved = moved_planes(planes, *taps, row_count, col_count)
        patches[tap_rows(0, *taps, chans), cells:] = moved[:, : span - cells]
        patches[tap_rows(1, *taps, chans)] = moved
        patches[tap_rows(2, *taps, chans), : span - cells] = moved[:, cells:]


def fill_outer(patches, edges, low, high, row_count, col_count):
    chans, cells = edges.shape[1:]
    span = patches.shape[1]
    first = (edges[0].astype(jnp.float32) * low).astype(jnp.bfloat16)
    last = (edges[1].astype(jnp.float32) * high).astype(jnp.bfloat16)
    planes = jnp.concatenate([first, last], axis=1)
    for taps in plane_taps():
        moved = moved_planes(planes, *taps, row_count, col_count)
        patches[tap_rows(0, *taps, chans), :cells] = moved[:, :cells]
        patches[tap_rows(2, *taps, chans), span - cells :] = moved[:, cells:]


def gelu_bend(values):
    return jnp.tanh(0.7978845608028654 * values * (1.0 + 0.044715 * values * values))


def gelu_slope(values, bend):
    outer = 0.7978845608028654 * (1.0 + 0.134145 * values * values)
    return 0.5 * (1.0 + bend) + 0.5 * values * (1.0 - bend * bend) * outer


def contract(left, right, left_dim, right_dim):
    return lax.dot_general(
        left, right, (((left_dim,), (right_dim,)), ((), ())), preferred_element_type=jnp.float32
    )


def pool_cells(values, row_count, col_count):
    cells = row_count * col_count
    pairs = [
        values[:, 2 * d * cells : (2 * d + 1) * cells] + values[:, (2 * d + 1) * cells : (2 * d + 2) * cells]
        for d in range(values.shape[1] // (2 * cells))
    ]
    paired = jnp.concatenate(pairs, axis=1)
    span = paired.shape[1]
    paired = paired + pltpu.roll(paired, span - 1, 1)
    paired = paired + pltpu.roll(paired, span - col_count, 1)
    small = cells // 4
    target = lax.broadcasted_iota(jnp.int32, (span, span // 4), 1)
    cell = target % small
    corner = (
        target // small * cells
        + cell // (col_count // 2) * (2 * col_count)
        + cell % (col_count // 2) * 2
    )
    here = lax.broadcasted_iota(jnp.int32, (span, span // 4), 0)
    picks = jnp.where(here == corner, 1.0, 0.0).astype(jnp.bfloat16)
    return contract((paired * 0.125).astype(jnp.bfloat16), picks, 1, 0).astype(jnp.bfloat16)


def spread_cells(values, row_count, col_count):
    cells = row_count * col_count
    chans, small_span = values.shape
    span = small_span * 8
    cell = lax.broadcasted_iota(jnp.int32, (small_span, span), 1)
    source = (
        cell // (2 * cells) * (cells // 4)
        + cell % cells // (2 * col_count) * (col_count // 2)
        + cell % col_count // 2
    )
    here = lax.broadcasted_iota(jnp.int32, (small_span, span), 0)
    copies = jnp.where(here == source, 1.0, 0.0).astype(jnp.bfloat16)
    high = values.astype(jnp.bfloat16)
    rest = values - high.astype(jnp.float32)
    middle = rest.astype(jnp.bfloat16)
    low = (rest - middle.astype(jnp.float32)).astype(jnp.bfloat16)
    wide = contract(jnp.concatenate([high, middle, low], axis=0), copies, 1, 0)
    return wide[:chans] + wide[chans : 2 * chans] + wide[2 * chans :]


def merged_planes(planes):
    wide = planes.astype(jnp.float32)
    parts = [wide[:, d, :] for d in range(planes.shape[1])]
    return jnp.concatenate(parts, axis=1).astype(planes.dtype)


def finish_kernel(scale, grad_in_ref, mid_ref, deep_ref, grad_in_out, mid_out, deep_out):
    half = mid_ref.shape[0]
    cells = grad_in_out.shape[2]
    packed = mid_ref[...].astype(jnp.float32) * scale
    mid_out[:half] = packed[:, : mid_out.shape[1]]
    mid_out[half:] = packed[:, mid_out.shape[1] :]
    deep_out[...] = deep_ref[...].astype(jnp.float32) * scale
    grad_in = grad_in_ref[...]
    planes = [grad_in[:, d * cells : (d + 1) * cells] for d in range(grad_in_out.shape[1])]
    grad_in_out[...] = jnp.stack(planes, axis=1).astype(jnp.bfloat16)


def block_kernel(plans, layout, *refs):
    refs = list(refs)

    def take(count):
        taken = refs[:count]
        del refs[:count]
        return taken

    source_ref, cot_ref, mid_ref, deep_ref = take(4)
    grad_in_ref, mid_out, deep_out = take(3)
    mid_patches, deep_patches, deep_back, mid_back, mid_flip, deep_flip = take(6)
    edges = [take(2) for _ in range(4)]
    edge_send, edge_recv = take(2)
    works = []
    for stages in plans:
        total, outgoing, gathered = take(3)
        landing = take(len(stages))
        works.append(Reduction(stages, total, outgoing, gathered, landing, take(2)))
    first, second, third = works
    row_count, col_count = layout
    cells = row_count * col_count
    small = cells // 4
    chans1 = source_ref.shape[0]
    chans2, chans3 = deep_ref.shape[0] // 27, deep_ref.shape[1]
    dp, space = lax.axis_index("dp"), lax.axis_index("space")
    slabs = lax.axis_size("space")
    low = jnp.where(space > 0, 1.0, 0.0)
    high = jnp.where(space < slabs - 1, 1.0, 0.0)

    def swap_start(index, planes, cells_here):
        leaving, arriving = edges[index]
        leaving[0] = planes[:, :cells_here]
        leaving[1] = planes[:, planes.shape[1] - cells_here :]
        made = []
        for side, other in ((0, lax.rem(space + slabs - 1, slabs)), (1, lax.rem(space + 1, slabs))):
            made.append(
                pltpu.make_async_remote_copy(
                    src_ref=leaving.at[side],
                    dst_ref=arriving.at[1 - side],
                    send_sem=edge_send.at[2 * index + side],
                    recv_sem=edge_recv.at[2 * index + side],
                    device_id=(dp, other),
                    device_id_type=pl.DeviceIdType.MESH,
                )
            )
            made[-1].start()
        return made

    def swap_finish(index, made, patches, row_count, col_count):
        for one in made:
            one.wait_recv()
        fill_outer(patches, edges[index][1], low, high, row_count, col_count)

    greet(plans[0])
    source = merged_planes(source_ref[...])
    swap0 = swap_start(0, source, cells)
    for tap in range(27):
        mid_flip[:, tap * chans2 : (tap + 1) * chans2] = mid_ref[(26 - tap) * chans1 : (27 - tap) * chans1]
        deep_flip[:, tap * chans3 : (tap + 1) * chans3] = deep_ref[(26 - tap) * chans2 : (27 - tap) * chans2]
    deep_rows = deep_ref.shape[0]
    cut = deep_rows // 2
    half = mid_out.shape[0]
    for work, used in ((first, cut), (second, deep_rows - cut), (third, half)):
        spare = work.total.shape[0] - used
        if spare:
            work.total[used:] = jnp.zeros((spare, LANES), jnp.float32)
    fill_inner(mid_patches, source, row_count, col_count)
    swap_finish(0, swap0, mid_patches, row_count, col_count)
    mid_pre = contract(mid_ref[...], mid_patches[...], 0, 0)
    mid_bend = gelu_bend(mid_pre)
    pooled = pool_cells(0.5 * mid_pre * (1.0 + mid_bend), row_count, col_count)
    swap1 = swap_start(1, pooled, small)
    fill_inner(deep_patches, pooled, row_count // 2, col_count // 2)
    upstream = cot_ref[...].astype(jnp.float32).T
    mid_slope = gelu_slope(mid_pre, mid_bend)
    swap_finish(1, swap1, deep_patches, row_count // 2, col_count // 2)
    deep_pre = contract(deep_ref[...], deep_patches[...], 0, 0)
    deep_grad = (upstream * gelu_slope(deep_pre, gelu_bend(deep_pre))).astype(jnp.bfloat16)
    swap2 = swap_start(2, deep_grad, small)
    first.total[:cut] = contract(deep_patches[:cut], deep_grad, 1, 1)
    first.scatter_start(0)
    second.total[: deep_rows - cut] = contract(deep_patches[cut:], deep_grad, 1, 1)
    second.scatter_start(0)
    fill_inner(deep_back, deep_grad, row_count // 2, col_count // 2)
    swap_finish(2, swap2, deep_back, row_count // 2, col_count // 2)
    back = contract(deep_flip[...], deep_back[...], 1, 0)
    mid_grad = (spread_cells(back, row_count, col_count) * 0.125 * mid_slope).astype(jnp.bfloat16)
    swap3 = swap_start(3, mid_grad, cells)
    depth = len(plans[0])

    def advance(work, index):
        work.scatter_finish(index)
        if index + 1 < depth:
            work.scatter_start(index + 1)
        else:
            work.gather_own()
            work.gather_start(depth - 1)

    def collect(work, index):
        work.gather_finish()
        if index:
            work.gather_start(index - 1)

    advance(first, 0)
    advance(second, 0)
    third.total[:half] = jnp.concatenate(
        [contract(mid_patches[:half], mid_grad, 1, 1), contract(mid_patches[half:], mid_grad, 1, 1)], axis=1
    )
    third.scatter_start(0)
    advance(first, 1)
    advance(second, 1)
    fill_inner(mid_back, mid_grad, row_count, col_count)
    swap_finish(3, swap3, mid_back, row_count, col_count)
    advance(third, 0)
    grad_in_ref[...] = contract(mid_flip[...], mid_back[...], 1, 0)
    for index in range(2, depth):
        advance(first, index)
        advance(second, index)
        advance(third, index - 1)
    collect(first, depth - 1)
    collect(second, depth - 1)
    advance(third, depth - 1)
    for index in reversed(range(depth - 1)):
        collect(first, index)
        collect(second, index)
        collect(third, index + 1)
    deep_out[:cut] = first.gathered[:cut]
    deep_out[cut:] = second.gathered[: deep_rows - cut]
    collect(third, 0)
    mid_out[...] = third.gathered[:half]
    for one in swap0 + swap1 + swap2 + swap3:
        one.wait_send()
    for work in works:
        work.drain()


def shards(activations, cotangent, weight_mid, weight_deep):
    samples, slabs = lax.axis_size("dp"), lax.axis_size("space")
    stages = group_stages(samples, slabs)
    plans = (stages, stages, stages)
    chans1, chans2, chans3 = weight_mid.shape[3], weight_mid.shape[4], weight_deep.shape[4]
    source = activations[0]
    upstream = jnp.transpose(cotangent[0], (1, 2, 0)).reshape(-1, chans3)
    mid_flat = weight_mid.reshape(-1, chans2)
    deep_flat = weight_deep.reshape(-1, chans3)
    cells, small = source.shape[1] * source.shape[2], upstream.shape[0]
    plane, small_plane = ROWS * COLS, ROWS * COLS // 4
    half_rows = reduction_rows(-(-deep_flat.shape[0] // 2), samples * slabs)
    mid_rows = reduction_rows(mid_flat.shape[0] // 2, samples * slabs)
    scratch = [
        pltpu.VMEM((27 * chans1, cells), jnp.bfloat16),
        pltpu.VMEM((27 * chans2, small), jnp.bfloat16),
        pltpu.VMEM((27 * chans3, small), jnp.bfloat16),
        pltpu.VMEM((27 * chans2, cells), jnp.bfloat16),
        pltpu.VMEM((chans1, 27 * chans2), jnp.bfloat16),
        pltpu.VMEM((chans2, 27 * chans3), jnp.bfloat16),
    ]
    for chans, width in ((chans1, plane), (chans2, small_plane), (chans3, small_plane), (chans2, plane)):
        scratch += [pltpu.VMEM((2, chans, width), jnp.bfloat16)] * 2
    scratch += [pltpu.SemaphoreType.DMA((8,)), pltpu.SemaphoreType.DMA((8,))]
    for plan, rows in zip(plans, (half_rows, half_rows, mid_rows)):
        scratch += reduction_scratch(plan, rows)
    room = 24 * 1024 * 1024 + 12 * LANES * (2 * half_rows + mid_rows)
    grad_in, mid_sum, deep_sum = pl.pallas_call(
        functools.partial(block_kernel, plans, (ROWS, COLS)),
        out_shape=[
            jax.ShapeDtypeStruct((chans1, cells), jnp.float32),
            jax.ShapeDtypeStruct((mid_flat.shape[0] // 2, LANES), jnp.bfloat16),
            jax.ShapeDtypeStruct(deep_flat.shape, jnp.bfloat16),
        ],
        in_specs=[pl.BlockSpec(memory_space=pltpu.VMEM)] * 4,
        out_specs=[pl.BlockSpec(memory_space=pltpu.VMEM)] * 3,
        scratch_shapes=scratch,
        compiler_params=pltpu.CompilerParams(
            collective_id=0, has_side_effects=True, vmem_limit_bytes=min(room, 56 * 1024 * 1024)
        ),
    )(source, upstream, mid_flat, deep_flat)
    grad_in, mid_sum, deep_sum = pl.pallas_call(
        functools.partial(finish_kernel, 1.0 / samples),
        out_shape=[
            jax.ShapeDtypeStruct(source.shape, jnp.bfloat16),
            jax.ShapeDtypeStruct(mid_flat.shape, jnp.float32),
            jax.ShapeDtypeStruct(deep_flat.shape, jnp.float32),
        ],
        in_specs=[pl.BlockSpec(memory_space=pltpu.VMEM)] * 3,
        out_specs=[pl.BlockSpec(memory_space=pltpu.VMEM)] * 3,
        compiler_params=pltpu.CompilerParams(vmem_limit_bytes=16 * 1024 * 1024),
    )(grad_in, mid_sum, deep_sum)
    return (
        grad_in.reshape(activations.shape),
        mid_sum.reshape(weight_mid.shape),
        deep_sum.reshape(weight_deep.shape),
    )


def solution(mesh):
    in_specs = (P("dp", None, "space", None), P("dp", None, "space", None), P(), P())
    out_specs = (P("dp", None, "space", None), P(), P())
    return jax.shard_map(shards, mesh=mesh, in_specs=in_specs, out_specs=out_specs, check_vma=False)
```

```python
import functools

import jax
import jax.numpy as jnp
from jax import lax
from jax.experimental import pallas as pl
from jax.experimental.pallas import tpu as pltpu
from jax.sharding import PartitionSpec as P

ROWS = 4
COLS = 64
LANES = 128
ROW_TILE = 16


def group_stages(samples, slabs):
    stages = [("space", slabs, 1)]
    stride = 1
    for size in (4, 4):
        if samples // stride % size == 0:
            stages.append(("dp", size, stride))
            stride *= size
    if samples // stride > 1:
        stages.append(("dp", samples // stride, stride))
    return stages


def joined_stages(stages):
    (_, slabs, _), (_, size, _) = stages[:2]
    return [("both", size * slabs, 1)] + stages[2:]


def place(axis, size, stride):
    if axis == "both":
        slabs = lax.axis_size("space")
        return lax.rem(lax.axis_index("dp"), size // slabs) * slabs + lax.axis_index("space")
    return lax.rem(lax.axis_index(axis) // stride, size)


def partner(axis, size, stride, step):
    own = place(axis, size, stride)
    other = lax.rem(own + step, size)
    dp, space = lax.axis_index("dp"), lax.axis_index("space")
    if axis == "space":
        return other, (dp, other)
    if axis == "both":
        slabs = lax.axis_size("space")
        return other, (dp + other // slabs - own // slabs, lax.rem(other, slabs))
    return other, (dp + (other - own) * stride, space)


def rows_at(start, count):
    return pl.ds(pl.multiple_of(start, ROW_TILE), count)


class Reduction:
    def __init__(self, stages, total, outgoing, gathered, landing, sems):
        self.stages, self.total, self.outgoing = stages, total, outgoing
        self.gathered, self.landing, self.sems = gathered, landing, sems
        self.start, self.length = 0, total.shape[0]
        self.starts, self.copies, self.sent, self.used = [], [], [], 0
        self.done = 0

    def copy(self, source, target, device):
        send, recv = self.sems
        made = pltpu.make_async_remote_copy(
            src_ref=source,
            dst_ref=target,
            send_sem=send.at[self.used],
            recv_sem=recv.at[self.used],
            device_id=device,
            device_id_type=pl.DeviceIdType.MESH,
        )
        self.used += 1
        made.start()
        self.copies.append(made)

    def scatter_start(self, index):
        axis, size, stride = self.stages[index]
        piece = self.length // size
        for step in range(1, size):
            other, device = partner(axis, size, stride, step)
            window = rows_at(self.start + other * piece, piece)
            self.outgoing[window] = self.total[window].astype(jnp.bfloat16)
            self.copy(self.outgoing.at[window], self.landing[index].at[step - 1], device)
        self.starts.append(self.start)
        self.start = self.start + place(axis, size, stride) * piece
        self.length = piece

    def scatter_finish(self, index):
        window = rows_at(self.start, self.length)
        value = self.total[window]
        for step, made in enumerate(self.copies):
            made.wait_recv()
            value = value + self.landing[index][step].astype(jnp.float32)
        self.total[window] = value
        self.sent += self.copies
        self.copies = []

    def gather_own(self):
        window = rows_at(self.start, self.length)
        self.gathered[window] = self.total[window].astype(jnp.bfloat16)

    def gather_start(self, index):
        axis, size, stride = self.stages[index]
        window = rows_at(self.start, self.length)
        for step in range(1, size):
            _, device = partner(axis, size, stride, step)
            self.copy(self.gathered.at[window], self.gathered.at[window], device)
        self.start = self.starts[index]
        self.length = self.length * size

    def gather_finish(self):
        for made in self.copies:
            made.wait_recv()
        self.sent += self.copies
        self.copies = []

    def step(self):
        depth = len(self.stages)
        index = self.done
        self.done += 1
        if index < depth:
            self.scatter_finish(index)
            if index + 1 < depth:
                self.scatter_start(index + 1)
                return
            self.gather_own()
            self.gather_start(depth - 1)
            return
        self.gather_finish()
        if index + 1 < 2 * depth:
            self.gather_start(2 * depth - 2 - index)

    def pending(self):
        return self.done < 2 * len(self.stages)

    def drain(self):
        for made in self.sent:
            made.wait_send()


def reduction_rows(rows, devices):
    return -(-rows // (devices * ROW_TILE)) * ROW_TILE * devices


def reduction_scratch(stages, rows):
    shapes = [
        pltpu.VMEM((rows, LANES), jnp.float32),
        pltpu.VMEM((rows, LANES), jnp.bfloat16),
        pltpu.VMEM((rows, LANES), jnp.bfloat16),
    ]
    length, count = rows, 0
    for _, size, _ in stages:
        length //= size
        count += 2 * (size - 1)
        shapes.append(pltpu.VMEM((size - 1, length, LANES), jnp.bfloat16))
    return shapes + [pltpu.SemaphoreType.DMA((count,)), pltpu.SemaphoreType.DMA((count,))]


def greet(stages):
    barrier = pltpu.get_barrier_semaphore()
    count = 0
    for axis, size, stride in stages:
        for step in range(1, size):
            _, device = partner(axis, size, stride, step)
            pl.semaphore_signal(barrier, inc=1, device_id=device, device_id_type=pl.DeviceIdType.MESH)
            count += 1
    pl.semaphore_wait(barrier, count)


def moved_planes(planes, row_tap, col_tap, row_count, col_count):
    offset = (row_tap - 1) * col_count + col_tap - 1
    if not offset:
        return planes
    total = planes.shape[1]
    lane = lax.broadcasted_iota(jnp.int32, (1, total), 1)
    col_at = lane % col_count + (col_tap - 1)
    row_at = lane // col_count % row_count + (row_tap - 1)
    inside = (row_at >= 0) & (row_at < row_count) & (col_at >= 0) & (col_at < col_count)
    keep = jnp.where(inside, 1.0, 0.0).astype(jnp.bfloat16)
    return pltpu.roll(planes, -offset % total, 1) * keep


def plane_taps():
    return [(row_tap, col_tap) for row_tap in range(3) for col_tap in range(3)]


def tap_rows(depth_tap, row_tap, col_tap, chans):
    tap = (depth_tap * 3 + row_tap) * 3 + col_tap
    return slice(tap * chans, (tap + 1) * chans)


def fill_inner(patches, planes, row_count, col_count):
    chans, span = planes.shape
    cells = row_count * col_count
    for taps in plane_taps():
        moved = moved_planes(planes, *taps, row_count, col_count)
        patches[tap_rows(0, *taps, chans), cells:] = moved[:, : span - cells]
        patches[tap_rows(1, *taps, chans)] = moved
        patches[tap_rows(2, *taps, chans), : span - cells] = moved[:, cells:]


def fill_outer(patches, edges, low, high, row_count, col_count):
    chans, cells = edges.shape[1:]
    span = patches.shape[1]
    first = (edges[0].astype(jnp.float32) * low).astype(jnp.bfloat16)
    last = (edges[1].astype(jnp.float32) * high).astype(jnp.bfloat16)
    planes = jnp.concatenate([first, last], axis=1)
    for taps in plane_taps():
        moved = moved_planes(planes, *taps, row_count, col_count)
        patches[tap_rows(0, *taps, chans), :cells] = moved[:, :cells]
        patches[tap_rows(2, *taps, chans), span - cells :] = moved[:, cells:]


def gelu_bend(values):
    return jnp.tanh(0.7978845608028654 * values * (1.0 + 0.044715 * values * values))


def gelu_slope(values, bend):
    outer = 0.7978845608028654 * (1.0 + 0.134145 * values * values)
    return 0.5 * (1.0 + bend) + 0.5 * values * (1.0 - bend * bend) * outer


def contract(left, right, left_dim, right_dim):
    return lax.dot_general(
        left, right, (((left_dim,), (right_dim,)), ((), ())), preferred_element_type=jnp.float32
    )


def pool_cells(values, row_count, col_count):
    cells = row_count * col_count
    pairs = [
        values[:, 2 * d * cells : (2 * d + 1) * cells] + values[:, (2 * d + 1) * cells : (2 * d + 2) * cells]
        for d in range(values.shape[1] // (2 * cells))
    ]
    paired = jnp.concatenate(pairs, axis=1)
    span = paired.shape[1]
    paired = paired + pltpu.roll(paired, span - 1, 1)
    paired = paired + pltpu.roll(paired, span - col_count, 1)
    small = cells // 4
    target = lax.broadcasted_iota(jnp.int32, (span, span // 4), 1)
    cell = target % small
    corner = (
        target // small * cells
        + cell // (col_count // 2) * (2 * col_count)
        + cell % (col_count // 2) * 2
    )
    here = lax.broadcasted_iota(jnp.int32, (span, span // 4), 0)
    picks = jnp.where(here == corner, 1.0, 0.0).astype(jnp.bfloat16)
    return contract((paired * 0.125).astype(jnp.bfloat16), picks, 1, 0).astype(jnp.bfloat16)


def spread_cells(values, row_count, col_count):
    cells = row_count * col_count
    chans, small_span = values.shape
    span = small_span * 8
    cell = lax.broadcasted_iota(jnp.int32, (small_span, span), 1)
    source = (
        cell // (2 * cells) * (cells // 4)
        + cell % cells // (2 * col_count) * (col_count // 2)
        + cell % col_count // 2
    )
    here = lax.broadcasted_iota(jnp.int32, (small_span, span), 0)
    copies = jnp.where(here == source, 1.0, 0.0).astype(jnp.bfloat16)
    high = values.astype(jnp.bfloat16)
    rest = values - high.astype(jnp.float32)
    middle = rest.astype(jnp.bfloat16)
    low = (rest - middle.astype(jnp.float32)).astype(jnp.bfloat16)
    wide = contract(jnp.concatenate([high, middle, low], axis=0), copies, 1, 0)
    return wide[:chans] + wide[chans : 2 * chans] + wide[2 * chans :]


def merged_planes(planes):
    wide = planes.astype(jnp.float32)
    parts = [wide[:, d, :] for d in range(planes.shape[1])]
    return jnp.concatenate(parts, axis=1).astype(planes.dtype)


def finish_kernel(scale, grad_in_ref, mid_ref, deep_ref, grad_in_out, mid_out, deep_out):
    half = mid_ref.shape[0]
    cells = grad_in_out.shape[2]
    packed = mid_ref[...].astype(jnp.float32) * scale
    mid_out[:half] = packed[:, : mid_out.shape[1]]
    mid_out[half:] = packed[:, mid_out.shape[1] :]
    deep_out[...] = deep_ref[...].astype(jnp.float32) * scale
    grad_in = grad_in_ref[...]
    planes = [grad_in[:, d * cells : (d + 1) * cells] for d in range(grad_in_out.shape[1])]
    grad_in_out[...] = jnp.stack(planes, axis=1).astype(jnp.bfloat16)


def block_kernel(plans, layout, *refs):
    refs = list(refs)

    def take(count):
        taken = refs[:count]
        del refs[:count]
        return taken

    inputs = take(4)
    grad_in_ref, mid_out, deep_out = take(3)
    mid_patches, deep_patches, deep_back, mid_back, mid_flip, deep_flip, mid_turned, deep_turned = take(8)
    held = take(4)
    load_sem = take(1)[0]
    edges = [take(2) for _ in range(4)]
    edge_send, edge_recv = take(2)
    works = []
    for stages in plans:
        total, outgoing, gathered = take(3)
        landing = take(len(stages))
        works.append(Reduction(stages, total, outgoing, gathered, landing, take(2)))
    first, second, third = works
    loads = [pltpu.make_async_copy(*pair, load_sem.at[at]) for at, pair in enumerate(zip(inputs, held))]
    for load in loads:
        load.start()
    source_ref, cot_ref, mid_ref, deep_ref = held
    row_count, col_count = layout
    cells = row_count * col_count
    small = cells // 4
    chans1 = source_ref.shape[0]
    chans2, chans3 = deep_ref.shape[0] // 27, deep_ref.shape[1]
    dp, space = lax.axis_index("dp"), lax.axis_index("space")
    slabs = lax.axis_size("space")
    low = jnp.where(space > 0, 1.0, 0.0)
    high = jnp.where(space < slabs - 1, 1.0, 0.0)

    def swap_start(index, planes, cells_here):
        leaving, arriving = edges[index]
        leaving[0] = planes[:, :cells_here]
        leaving[1] = planes[:, planes.shape[1] - cells_here :]
        made = []
        for side, other in ((0, lax.rem(space + slabs - 1, slabs)), (1, lax.rem(space + 1, slabs))):
            made.append(
                pltpu.make_async_remote_copy(
                    src_ref=leaving.at[side],
                    dst_ref=arriving.at[1 - side],
                    send_sem=edge_send.at[2 * index + side],
                    recv_sem=edge_recv.at[2 * index + side],
                    device_id=(dp, other),
                    device_id_type=pl.DeviceIdType.MESH,
                )
            )
            made[-1].start()
        return made

    def swap_finish(index, made, patches, row_count, col_count):
        for one in made:
            one.wait_recv()
        fill_outer(patches, edges[index][1], low, high, row_count, col_count)

    greet(plans[2])
    loads[0].wait()
    source = merged_planes(source_ref[...])
    swap0 = swap_start(0, source, cells)
    deep_rows = deep_ref.shape[0]
    cut = deep_rows // 2
    half = mid_out.shape[0]
    for work, used in ((first, cut), (second, deep_rows - cut), (third, half)):
        spare = work.total.shape[0] - used
        if spare:
            work.total[used:] = jnp.zeros((spare, LANES), jnp.float32)
    fill_inner(mid_patches, source, row_count, col_count)
    loads[2].wait()
    mid_turned[...] = mid_ref[...].T
    swap_finish(0, swap0, mid_patches, row_count, col_count)
    mid_pre = contract(mid_turned[...], mid_patches[...], 1, 0)
    mid_bend = gelu_bend(mid_pre)
    pooled = pool_cells(0.5 * mid_pre * (1.0 + mid_bend), row_count, col_count)
    swap1 = swap_start(1, pooled, small)
    fill_inner(deep_patches, pooled, row_count // 2, col_count // 2)
    loads[3].wait()
    deep_turned[...] = deep_ref[...].T
    loads[1].wait()
    upstream = cot_ref[...].astype(jnp.float32).T
    mid_slope = gelu_slope(mid_pre, mid_bend)
    swap_finish(1, swap1, deep_patches, row_count // 2, col_count // 2)
    deep_pre = contract(deep_turned[...], deep_patches[...], 1, 0)
    deep_grad = (upstream * gelu_slope(deep_pre, gelu_bend(deep_pre))).astype(jnp.bfloat16)
    swap2 = swap_start(2, deep_grad, small)
    first.total[:cut] = contract(deep_patches[:cut], deep_grad, 1, 1)
    first.scatter_start(0)
    second.total[: deep_rows - cut] = contract(deep_patches[cut:], deep_grad, 1, 1)
    second.scatter_start(0)
    fill_inner(deep_back, deep_grad, row_count // 2, col_count // 2)
    for tap in range(27):
        deep_flip[:, tap * chans3 : (tap + 1) * chans3] = deep_ref[(26 - tap) * chans2 : (27 - tap) * chans2]
    swap_finish(2, swap2, deep_back, row_count // 2, col_count // 2)
    back = contract(deep_flip[...], deep_back[...], 1, 0)
    mid_grad = (spread_cells(back, row_count, col_count) * 0.125 * mid_slope).astype(jnp.bfloat16)
    swap3 = swap_start(3, mid_grad, cells)
    first.step()
    second.step()
    third.total[:half] = jnp.concatenate(
        [contract(mid_patches[:half], mid_grad, 1, 1), contract(mid_patches[half:], mid_grad, 1, 1)], axis=1
    )
    third.scatter_start(0)
    first.step()
    second.step()
    fill_inner(mid_back, mid_grad, row_count, col_count)
    for tap in range(27):
        mid_flip[:, tap * chans2 : (tap + 1) * chans2] = mid_ref[(26 - tap) * chans1 : (27 - tap) * chans1]
    swap_finish(3, swap3, mid_back, row_count, col_count)
    third.step()
    grad_in_ref[...] = contract(mid_flip[...], mid_back[...], 1, 0)
    while any(work.pending() for work in works):
        for work in works:
            if work.pending():
                work.step()
    deep_out[:cut] = first.gathered[:cut]
    deep_out[cut:] = second.gathered[: deep_rows - cut]
    mid_out[...] = third.gathered[:half]
    for one in swap0 + swap1 + swap2 + swap3:
        one.wait_send()
    for work in works:
        work.drain()


def shards(activations, cotangent, weight_mid, weight_deep):
    samples, slabs = lax.axis_size("dp"), lax.axis_size("space")
    stages = group_stages(samples, slabs)
    turned = stages[:1] + stages[1:][::-1]
    plans = (stages, turned, joined_stages(stages))
    chans1, chans2, chans3 = weight_mid.shape[3], weight_mid.shape[4], weight_deep.shape[4]
    source = activations[0]
    upstream = jnp.transpose(cotangent[0], (1, 2, 0)).reshape(-1, chans3)
    mid_flat = weight_mid.reshape(-1, chans2)
    deep_flat = weight_deep.reshape(-1, chans3)
    cells, small = source.shape[1] * source.shape[2], upstream.shape[0]
    plane, small_plane = ROWS * COLS, ROWS * COLS // 4
    half_rows = reduction_rows(-(-deep_flat.shape[0] // 2), samples * slabs)
    mid_rows = reduction_rows(mid_flat.shape[0] // 2, samples * slabs)
    scratch = [
        pltpu.VMEM((27 * chans1, cells), jnp.bfloat16),
        pltpu.VMEM((27 * chans2, small), jnp.bfloat16),
        pltpu.VMEM((27 * chans3, small), jnp.bfloat16),
        pltpu.VMEM((27 * chans2, cells), jnp.bfloat16),
        pltpu.VMEM((chans1, 27 * chans2), jnp.bfloat16),
        pltpu.VMEM((chans2, 27 * chans3), jnp.bfloat16),
        pltpu.VMEM(mid_flat.shape[::-1], jnp.bfloat16),
        pltpu.VMEM(deep_flat.shape[::-1], jnp.bfloat16),
        *(pltpu.VMEM(one.shape, jnp.bfloat16) for one in (source, upstream, mid_flat, deep_flat)),
        pltpu.SemaphoreType.DMA((4,)),
    ]
    for chans, width in ((chans1, plane), (chans2, small_plane), (chans3, small_plane), (chans2, plane)):
        scratch += [pltpu.VMEM((2, chans, width), jnp.bfloat16)] * 2
    scratch += [pltpu.SemaphoreType.DMA((8,)), pltpu.SemaphoreType.DMA((8,))]
    for plan, rows in zip(plans, (half_rows, half_rows, mid_rows)):
        scratch += reduction_scratch(plan, rows)
    room = 24 * 1024 * 1024 + 12 * LANES * (2 * half_rows + mid_rows)
    grad_in, mid_sum, deep_sum = pl.pallas_call(
        functools.partial(block_kernel, plans, (ROWS, COLS)),
        out_shape=[
            jax.ShapeDtypeStruct((chans1, cells), jnp.float32),
            jax.ShapeDtypeStruct((mid_flat.shape[0] // 2, LANES), jnp.bfloat16),
            jax.ShapeDtypeStruct(deep_flat.shape, jnp.bfloat16),
        ],
        in_specs=[pl.BlockSpec(memory_space=pltpu.HBM)] * 4,
        out_specs=[pl.BlockSpec(memory_space=pltpu.VMEM)] * 3,
        scratch_shapes=scratch,
        compiler_params=pltpu.CompilerParams(
            collective_id=0, has_side_effects=True, vmem_limit_bytes=min(room, 56 * 1024 * 1024)
        ),
    )(source, upstream, mid_flat, deep_flat)
    grad_in, mid_sum, deep_sum = pl.pallas_call(
        functools.partial(finish_kernel, 1.0 / samples),
        out_shape=[
            jax.ShapeDtypeStruct(source.shape, jnp.bfloat16),
            jax.ShapeDtypeStruct(mid_flat.shape, jnp.float32),
            jax.ShapeDtypeStruct(deep_flat.shape, jnp.float32),
        ],
        in_specs=[pl.BlockSpec(memory_space=pltpu.VMEM)] * 3,
        out_specs=[pl.BlockSpec(memory_space=pltpu.VMEM)] * 3,
        compiler_params=pltpu.CompilerParams(vmem_limit_bytes=16 * 1024 * 1024),
    )(grad_in, mid_sum, deep_sum)
    return (
        grad_in.reshape(activations.shape),
        mid_sum.reshape(weight_mid.shape),
        deep_sum.reshape(weight_deep.shape),
    )


def solution(mesh):
    in_specs = (P("dp", None, "space", None), P("dp", None, "space", None), P(), P())
    out_specs = (P("dp", None, "space", None), P(), P())
    return jax.shard_map(shards, mesh=mesh, in_specs=in_specs, out_specs=out_specs, check_vma=False)
```

```python
import functools

import jax
import jax.numpy as jnp
from jax import lax
from jax.experimental import pallas as pl
from jax.experimental.pallas import tpu as pltpu
from jax.sharding import PartitionSpec as P

ROWS = 4
COLS = 64
LANES = 128
ROW_TILE = 16


def group_stages(samples, slabs):
    stages = [("space", slabs, 1)]
    stride = 1
    for size in (4, 4):
        if samples // stride % size == 0:
            stages.append(("dp", size, stride))
            stride *= size
    if samples // stride > 1:
        stages.append(("dp", samples // stride, stride))
    return stages


def joined_stages(stages):
    (_, slabs, _), (_, size, _) = stages[:2]
    return [("both", size * slabs, 1)] + stages[2:]


def place(axis, size, stride):
    if axis == "both":
        slabs = lax.axis_size("space")
        return lax.rem(lax.axis_index("dp"), size // slabs) * slabs + lax.axis_index("space")
    return lax.rem(lax.axis_index(axis) // stride, size)


def partner(axis, size, stride, step):
    own = place(axis, size, stride)
    other = lax.rem(own + step, size)
    dp, space = lax.axis_index("dp"), lax.axis_index("space")
    if axis == "space":
        return other, (dp, other)
    if axis == "both":
        slabs = lax.axis_size("space")
        return other, (dp + other // slabs - own // slabs, lax.rem(other, slabs))
    return other, (dp + (other - own) * stride, space)


def rows_at(start, count):
    return pl.ds(pl.multiple_of(start, ROW_TILE), count)


class Reduction:
    def __init__(self, stages, total, outgoing, gathered, landing, sems):
        self.stages, self.total, self.outgoing = stages, total, outgoing
        self.gathered, self.landing, self.sems = gathered, landing, sems
        self.start, self.length = 0, total.shape[0]
        self.starts, self.copies, self.sent, self.used = [], [], [], 0
        self.done = 0

    def copy(self, source, target, device):
        send, recv = self.sems
        made = pltpu.make_async_remote_copy(
            src_ref=source,
            dst_ref=target,
            send_sem=send.at[self.used],
            recv_sem=recv.at[self.used],
            device_id=device,
            device_id_type=pl.DeviceIdType.MESH,
        )
        self.used += 1
        made.start()
        self.copies.append(made)

    def scatter_start(self, index):
        axis, size, stride = self.stages[index]
        piece = self.length // size
        for step in range(1, size):
            other, device = partner(axis, size, stride, step)
            window = rows_at(self.start + other * piece, piece)
            self.outgoing[window] = self.total[window].astype(jnp.bfloat16)
            self.copy(self.outgoing.at[window], self.landing[index].at[step - 1], device)
        self.starts.append(self.start)
        self.start = self.start + place(axis, size, stride) * piece
        self.length = piece

    def scatter_finish(self, index):
        window = rows_at(self.start, self.length)
        value = self.total[window]
        for step, made in enumerate(self.copies):
            made.wait_recv()
            value = value + self.landing[index][step].astype(jnp.float32)
        self.total[window] = value
        self.sent += self.copies
        self.copies = []

    def gather_own(self):
        window = rows_at(self.start, self.length)
        self.gathered[window] = self.total[window].astype(jnp.bfloat16)

    def gather_start(self, index):
        axis, size, stride = self.stages[index]
        window = rows_at(self.start, self.length)
        for step in range(1, size):
            _, device = partner(axis, size, stride, step)
            self.copy(self.gathered.at[window], self.gathered.at[window], device)
        self.start = self.starts[index]
        self.length = self.length * size

    def gather_finish(self):
        for made in self.copies:
            made.wait_recv()
        self.sent += self.copies
        self.copies = []

    def step(self):
        depth = len(self.stages)
        index = self.done
        self.done += 1
        if index < depth:
            self.scatter_finish(index)
            if index + 1 < depth:
                self.scatter_start(index + 1)
                return
            self.gather_own()
            self.gather_start(depth - 1)
            return
        self.gather_finish()
        if index + 1 < 2 * depth:
            self.gather_start(2 * depth - 2 - index)

    def pending(self):
        return self.done < 2 * len(self.stages)

    def drain(self):
        for made in self.sent:
            made.wait_send()


def reduction_rows(rows, devices):
    return -(-rows // (devices * ROW_TILE)) * ROW_TILE * devices


def reduction_scratch(stages, rows):
    shapes = [
        pltpu.VMEM((rows, LANES), jnp.float32),
        pltpu.VMEM((rows, LANES), jnp.bfloat16),
        pltpu.VMEM((rows, LANES), jnp.bfloat16),
    ]
    length, count = rows, 0
    for _, size, _ in stages:
        length //= size
        count += 2 * (size - 1)
        shapes.append(pltpu.VMEM((size - 1, length, LANES), jnp.bfloat16))
    return shapes + [pltpu.SemaphoreType.DMA((count,)), pltpu.SemaphoreType.DMA((count,))]


def greet(stages):
    barrier = pltpu.get_barrier_semaphore()
    count = 0
    for axis, size, stride in stages:
        for step in range(1, size):
            _, device = partner(axis, size, stride, step)
            pl.semaphore_signal(barrier, inc=1, device_id=device, device_id_type=pl.DeviceIdType.MESH)
            count += 1
    return count


def moved_planes(planes, row_tap, col_tap, row_count, col_count):
    offset = (row_tap - 1) * col_count + col_tap - 1
    if not offset:
        return planes
    total = planes.shape[1]
    lane = lax.broadcasted_iota(jnp.int32, (1, total), 1)
    col_at = lane % col_count + (col_tap - 1)
    row_at = lane // col_count % row_count + (row_tap - 1)
    inside = (row_at >= 0) & (row_at < row_count) & (col_at >= 0) & (col_at < col_count)
    keep = jnp.where(inside, 1.0, 0.0).astype(jnp.bfloat16)
    return pltpu.roll(planes, -offset % total, 1) * keep


def plane_taps():
    return [(row_tap, col_tap) for row_tap in range(3) for col_tap in range(3)]


def tap_rows(depth_tap, row_tap, col_tap, chans):
    tap = (depth_tap * 3 + row_tap) * 3 + col_tap
    return slice(tap * chans, (tap + 1) * chans)


def fill_inner(patches, planes, row_count, col_count):
    chans, span = planes.shape
    cells = row_count * col_count
    for taps in plane_taps():
        moved = moved_planes(planes, *taps, row_count, col_count)
        patches[tap_rows(0, *taps, chans), cells:] = moved[:, : span - cells]
        patches[tap_rows(1, *taps, chans)] = moved
        patches[tap_rows(2, *taps, chans), : span - cells] = moved[:, cells:]


def fill_outer(patches, edges, low, high, row_count, col_count):
    chans, cells = edges.shape[1:]
    span = patches.shape[1]
    first = (edges[0].astype(jnp.float32) * low).astype(jnp.bfloat16)
    last = (edges[1].astype(jnp.float32) * high).astype(jnp.bfloat16)
    planes = jnp.concatenate([first, last], axis=1)
    for taps in plane_taps():
        moved = moved_planes(planes, *taps, row_count, col_count)
        patches[tap_rows(0, *taps, chans), :cells] = moved[:, :cells]
        patches[tap_rows(2, *taps, chans), span - cells :] = moved[:, cells:]


def gelu_bend(values):
    return jnp.tanh(0.7978845608028654 * values * (1.0 + 0.044715 * values * values))


def gelu_slope(values, bend):
    outer = 0.7978845608028654 * (1.0 + 0.134145 * values * values)
    return 0.5 * (1.0 + bend) + 0.5 * values * (1.0 - bend * bend) * outer


def contract(left, right, left_dim, right_dim):
    return lax.dot_general(
        left, right, (((left_dim,), (right_dim,)), ((), ())), preferred_element_type=jnp.float32
    )


def pool_cells(values, row_count, col_count):
    cells = row_count * col_count
    pairs = [
        values[:, 2 * d * cells : (2 * d + 1) * cells] + values[:, (2 * d + 1) * cells : (2 * d + 2) * cells]
        for d in range(values.shape[1] // (2 * cells))
    ]
    paired = jnp.concatenate(pairs, axis=1)
    span = paired.shape[1]
    paired = paired + pltpu.roll(paired, span - 1, 1)
    paired = paired + pltpu.roll(paired, span - col_count, 1)
    small = cells // 4
    target = lax.broadcasted_iota(jnp.int32, (span, span // 4), 1)
    cell = target % small
    corner = (
        target // small * cells
        + cell // (col_count // 2) * (2 * col_count)
        + cell % (col_count // 2) * 2
    )
    here = lax.broadcasted_iota(jnp.int32, (span, span // 4), 0)
    picks = jnp.where(here == corner, 1.0, 0.0).astype(jnp.bfloat16)
    return contract((paired * 0.125).astype(jnp.bfloat16), picks, 1, 0).astype(jnp.bfloat16)


def spread_cells(values, row_count, col_count):
    cells = row_count * col_count
    chans, small_span = values.shape
    span = small_span * 8
    cell = lax.broadcasted_iota(jnp.int32, (small_span, span), 1)
    source = (
        cell // (2 * cells) * (cells // 4)
        + cell % cells // (2 * col_count) * (col_count // 2)
        + cell % col_count // 2
    )
    here = lax.broadcasted_iota(jnp.int32, (small_span, span), 0)
    copies = jnp.where(here == source, 1.0, 0.0).astype(jnp.bfloat16)
    high = values.astype(jnp.bfloat16)
    rest = values - high.astype(jnp.float32)
    middle = rest.astype(jnp.bfloat16)
    low = (rest - middle.astype(jnp.float32)).astype(jnp.bfloat16)
    wide = contract(jnp.concatenate([high, middle, low], axis=0), copies, 1, 0)
    return wide[:chans] + wide[chans : 2 * chans] + wide[2 * chans :]


def merged_planes(planes):
    wide = planes.astype(jnp.float32)
    parts = [wide[:, d, :] for d in range(planes.shape[1])]
    return jnp.concatenate(parts, axis=1).astype(planes.dtype)


def finish_kernel(scale, grad_in_ref, mid_ref, deep_ref, grad_in_out, mid_out, deep_out):
    half = mid_ref.shape[0]
    cells = grad_in_out.shape[2]
    packed = mid_ref[...].astype(jnp.float32) * scale
    mid_out[:half] = packed[:, : mid_out.shape[1]]
    mid_out[half:] = packed[:, mid_out.shape[1] :]
    deep_out[...] = deep_ref[...].astype(jnp.float32) * scale
    grad_in = grad_in_ref[...]
    planes = [grad_in[:, d * cells : (d + 1) * cells] for d in range(grad_in_out.shape[1])]
    grad_in_out[...] = jnp.stack(planes, axis=1).astype(jnp.bfloat16)


def block_kernel(plans, layout, *refs):
    refs = list(refs)

    def take(count):
        taken = refs[:count]
        del refs[:count]
        return taken

    inputs = take(4)
    grad_in_ref, mid_out, deep_out = take(3)
    mid_patches, deep_patches, deep_back, mid_back, mid_flip, deep_flip, mid_turned, deep_turned = take(8)
    held = take(4)
    load_sem = take(1)[0]
    edges = [take(2) for _ in range(4)]
    edge_send, edge_recv = take(2)
    works = []
    for stages in plans:
        total, outgoing, gathered = take(3)
        landing = take(len(stages))
        works.append(Reduction(stages, total, outgoing, gathered, landing, take(2)))
    first, second, third = works
    loads = [pltpu.make_async_copy(*pair, load_sem.at[at]) for at, pair in enumerate(zip(inputs, held))]
    for load in loads:
        load.start()
    source_ref, cot_ref, mid_ref, deep_ref = held
    row_count, col_count = layout
    cells = row_count * col_count
    small = cells // 4
    chans1 = source_ref.shape[0]
    chans2, chans3 = deep_ref.shape[0] // 27, deep_ref.shape[1]
    dp, space = lax.axis_index("dp"), lax.axis_index("space")
    slabs = lax.axis_size("space")
    low = jnp.where(space > 0, 1.0, 0.0)
    high = jnp.where(space < slabs - 1, 1.0, 0.0)

    def swap_start(index, planes, cells_here):
        leaving, arriving = edges[index]
        if planes is not None:
            leaving[0] = planes[:, :cells_here]
            leaving[1] = planes[:, planes.shape[1] - cells_here :]
        made = []
        for side, other in ((0, lax.rem(space + slabs - 1, slabs)), (1, lax.rem(space + 1, slabs))):
            made.append(
                pltpu.make_async_remote_copy(
                    src_ref=leaving.at[side],
                    dst_ref=arriving.at[1 - side],
                    send_sem=edge_send.at[2 * index + side],
                    recv_sem=edge_recv.at[2 * index + side],
                    device_id=(dp, other),
                    device_id_type=pl.DeviceIdType.MESH,
                )
            )
            made[-1].start()
        return made

    def swap_finish(index, made, patches, row_count, col_count):
        for one in made:
            one.wait_recv()
        fill_outer(patches, edges[index][1], low, high, row_count, col_count)

    greeted = greet(plans[2])
    loads[0].wait()
    source = merged_planes(source_ref[...])
    edges[0][0][0] = source[:, :cells]
    edges[0][0][1] = source[:, source.shape[1] - cells :]
    pl.semaphore_wait(pltpu.get_barrier_semaphore(), greeted)
    swap0 = swap_start(0, None, cells)
    deep_rows = deep_ref.shape[0]
    cut = deep_rows // 2
    half = mid_out.shape[0]
    for work, used in ((first, cut), (second, deep_rows - cut), (third, half)):
        spare = work.total.shape[0] - used
        if spare:
            work.total[used:] = jnp.zeros((spare, LANES), jnp.float32)
    fill_inner(mid_patches, source, row_count, col_count)
    loads[2].wait()
    mid_turned[...] = mid_ref[...].T
    swap_finish(0, swap0, mid_patches, row_count, col_count)
    mid_pre = contract(mid_turned[...], mid_patches[...], 1, 0)
    mid_bend = gelu_bend(mid_pre)
    pooled = pool_cells(0.5 * mid_pre * (1.0 + mid_bend), row_count, col_count)
    swap1 = swap_start(1, pooled, small)
    fill_inner(deep_patches, pooled, row_count // 2, col_count // 2)
    loads[3].wait()
    deep_turned[...] = deep_ref[...].T
    loads[1].wait()
    upstream = cot_ref[...].astype(jnp.float32).T
    mid_slope = gelu_slope(mid_pre, mid_bend)
    swap_finish(1, swap1, deep_patches, row_count // 2, col_count // 2)
    deep_pre = contract(deep_turned[...], deep_patches[...], 1, 0)
    deep_grad = (upstream * gelu_slope(deep_pre, gelu_bend(deep_pre))).astype(jnp.bfloat16)
    swap2 = swap_start(2, deep_grad, small)
    first.total[:cut] = contract(deep_patches[:cut], deep_grad, 1, 1)
    first.scatter_start(0)
    second.total[: deep_rows - cut] = contract(deep_patches[cut:], deep_grad, 1, 1)
    second.scatter_start(0)
    fill_inner(deep_back, deep_grad, row_count // 2, col_count // 2)
    for tap in range(27):
        deep_flip[:, tap * chans3 : (tap + 1) * chans3] = deep_ref[(26 - tap) * chans2 : (27 - tap) * chans2]
    swap_finish(2, swap2, deep_back, row_count // 2, col_count // 2)
    back = contract(deep_flip[...], deep_back[...], 1, 0)
    mid_grad = (spread_cells(back, row_count, col_count) * 0.125 * mid_slope).astype(jnp.bfloat16)
    swap3 = swap_start(3, mid_grad, cells)
    first.step()
    second.step()
    third.total[:half] = jnp.concatenate(
        [contract(mid_patches[:half], mid_grad, 1, 1), contract(mid_patches[half:], mid_grad, 1, 1)], axis=1
    )
    third.scatter_start(0)
    fill_inner(mid_back, mid_grad, row_count, col_count)
    first.step()
    second.step()
    for tap in range(27):
        mid_flip[:, tap * chans2 : (tap + 1) * chans2] = mid_ref[(26 - tap) * chans1 : (27 - tap) * chans1]
    swap_finish(3, swap3, mid_back, row_count, col_count)
    third.step()
    grad_in_ref[...] = contract(mid_flip[...], mid_back[...], 1, 0)
    while any(work.pending() for work in works):
        for work in works:
            if work.pending():
                work.step()
    deep_out[:cut] = first.gathered[:cut]
    deep_out[cut:] = second.gathered[: deep_rows - cut]
    mid_out[...] = third.gathered[:half]
    for one in swap0 + swap1 + swap2 + swap3:
        one.wait_send()
    for work in works:
        work.drain()


def shards(activations, cotangent, weight_mid, weight_deep):
    samples, slabs = lax.axis_size("dp"), lax.axis_size("space")
    stages = group_stages(samples, slabs)
    turned = stages[:1] + stages[1:][::-1]
    plans = (stages, turned, joined_stages(stages))
    chans1, chans2, chans3 = weight_mid.shape[3], weight_mid.shape[4], weight_deep.shape[4]
    source = activations[0]
    upstream = jnp.transpose(cotangent[0], (1, 2, 0)).reshape(-1, chans3)
    mid_flat = weight_mid.reshape(-1, chans2)
    deep_flat = weight_deep.reshape(-1, chans3)
    cells, small = source.shape[1] * source.shape[2], upstream.shape[0]
    plane, small_plane = ROWS * COLS, ROWS * COLS // 4
    half_rows = reduction_rows(-(-deep_flat.shape[0] // 2), samples * slabs)
    mid_rows = reduction_rows(mid_flat.shape[0] // 2, samples * slabs)
    scratch = [
        pltpu.VMEM((27 * chans1, cells), jnp.bfloat16),
        pltpu.VMEM((27 * chans2, small), jnp.bfloat16),
        pltpu.VMEM((27 * chans3, small), jnp.bfloat16),
        pltpu.VMEM((27 * chans2, cells), jnp.bfloat16),
        pltpu.VMEM((chans1, 27 * chans2), jnp.bfloat16),
        pltpu.VMEM((chans2, 27 * chans3), jnp.bfloat16),
        pltpu.VMEM(mid_flat.shape[::-1], jnp.bfloat16),
        pltpu.VMEM(deep_flat.shape[::-1], jnp.bfloat16),
        *(pltpu.VMEM(one.shape, jnp.bfloat16) for one in (source, upstream, mid_flat, deep_flat)),
        pltpu.SemaphoreType.DMA((4,)),
    ]
    for chans, width in ((chans1, plane), (chans2, small_plane), (chans3, small_plane), (chans2, plane)):
        scratch += [pltpu.VMEM((2, chans, width), jnp.bfloat16)] * 2
    scratch += [pltpu.SemaphoreType.DMA((8,)), pltpu.SemaphoreType.DMA((8,))]
    for plan, rows in zip(plans, (half_rows, half_rows, mid_rows)):
        scratch += reduction_scratch(plan, rows)
    grad_in, mid_sum, deep_sum = pl.pallas_call(
        functools.partial(block_kernel, plans, (ROWS, COLS)),
        out_shape=[
            jax.ShapeDtypeStruct((chans1, cells), jnp.float32),
            jax.ShapeDtypeStruct((mid_flat.shape[0] // 2, LANES), jnp.bfloat16),
            jax.ShapeDtypeStruct(deep_flat.shape, jnp.bfloat16),
        ],
        in_specs=[pl.BlockSpec(memory_space=pltpu.HBM)] * 4,
        out_specs=[pl.BlockSpec(memory_space=pltpu.VMEM)] * 3,
        scratch_shapes=scratch,
        compiler_params=pltpu.CompilerParams(
            collective_id=0, has_side_effects=True, vmem_limit_bytes=56 * 1024 * 1024
        ),
    )(source, upstream, mid_flat, deep_flat)
    grad_in, mid_sum, deep_sum = pl.pallas_call(
        functools.partial(finish_kernel, 1.0 / samples),
        out_shape=[
            jax.ShapeDtypeStruct(source.shape, jnp.bfloat16),
            jax.ShapeDtypeStruct(mid_flat.shape, jnp.float32),
            jax.ShapeDtypeStruct(deep_flat.shape, jnp.float32),
        ],
        in_specs=[pl.BlockSpec(memory_space=pltpu.VMEM)] * 3,
        out_specs=[pl.BlockSpec(memory_space=pltpu.VMEM)] * 3,
        compiler_params=pltpu.CompilerParams(vmem_limit_bytes=56 * 1024 * 1024),
    )(grad_in, mid_sum, deep_sum)
    return (
        grad_in.reshape(activations.shape),
        mid_sum.reshape(weight_mid.shape),
        deep_sum.reshape(weight_deep.shape),
    )


def solution(mesh):
    in_specs = (P("dp", None, "space", None), P("dp", None, "space", None), P(), P())
    out_specs = (P("dp", None, "space", None), P(), P())
    return jax.shard_map(shards, mesh=mesh, in_specs=in_specs, out_specs=out_specs, check_vma=False)
```

```python
import functools

import jax
import jax.numpy as jnp
from jax import lax
from jax.experimental import pallas as pl
from jax.experimental.pallas import tpu as pltpu
from jax.sharding import PartitionSpec as P

ROWS = 4
COLS = 64
LANES = 128
ROW_TILE = 16


def group_stages(samples, slabs):
    stages = [("space", slabs, 1)]
    stride = 1
    for size in (4, 4):
        if samples // stride % size == 0:
            stages.append(("dp", size, stride))
            stride *= size
    if samples // stride > 1:
        stages.append(("dp", samples // stride, stride))
    return stages


def joined_stages(stages):
    (_, slabs, _), (_, size, _) = stages[:2]
    return [("both", size * slabs, 1)] + stages[2:]


def place(axis, size, stride):
    if axis == "both":
        slabs = lax.axis_size("space")
        return lax.rem(lax.axis_index("dp"), size // slabs) * slabs + lax.axis_index("space")
    return lax.rem(lax.axis_index(axis) // stride, size)


def partner(axis, size, stride, step):
    own = place(axis, size, stride)
    other = lax.rem(own + step, size)
    dp, space = lax.axis_index("dp"), lax.axis_index("space")
    if axis == "space":
        return other, (dp, other)
    if axis == "both":
        slabs = lax.axis_size("space")
        return other, (dp + other // slabs - own // slabs, lax.rem(other, slabs))
    return other, (dp + (other - own) * stride, space)


def rows_at(start, count):
    return pl.ds(pl.multiple_of(start, ROW_TILE), count)


class Reduction:
    def __init__(self, stages, total, outgoing, gathered, landing, sems):
        self.stages, self.total, self.outgoing = stages, total, outgoing
        self.gathered, self.landing, self.sems = gathered, landing, sems
        self.start, self.length = 0, total.shape[0]
        self.starts, self.copies, self.sent, self.used = [], [], [], 0
        self.done = 0

    def copy(self, source, target, device):
        send, recv = self.sems
        made = pltpu.make_async_remote_copy(
            src_ref=source,
            dst_ref=target,
            send_sem=send.at[self.used],
            recv_sem=recv.at[self.used],
            device_id=device,
            device_id_type=pl.DeviceIdType.MESH,
        )
        self.used += 1
        made.start()
        self.copies.append(made)

    def scatter_start(self, index):
        axis, size, stride = self.stages[index]
        piece = self.length // size
        for step in range(1, size):
            other, device = partner(axis, size, stride, step)
            window = rows_at(self.start + other * piece, piece)
            self.outgoing[window] = self.total[window].astype(jnp.bfloat16)
            self.copy(self.outgoing.at[window], self.landing[index].at[step - 1], device)
        self.starts.append(self.start)
        self.start = self.start + place(axis, size, stride) * piece
        self.length = piece

    def scatter_finish(self, index):
        window = rows_at(self.start, self.length)
        value = self.total[window]
        for step, made in enumerate(self.copies):
            made.wait_recv()
            value = value + self.landing[index][step].astype(jnp.float32)
        self.total[window] = value
        self.sent += self.copies
        self.copies = []

    def gather_own(self):
        window = rows_at(self.start, self.length)
        self.gathered[window] = self.total[window].astype(jnp.bfloat16)

    def gather_start(self, index):
        axis, size, stride = self.stages[index]
        window = rows_at(self.start, self.length)
        for step in range(1, size):
            _, device = partner(axis, size, stride, step)
            self.copy(self.gathered.at[window], self.gathered.at[window], device)
        self.start = self.starts[index]
        self.length = self.length * size

    def gather_finish(self):
        for made in self.copies:
            made.wait_recv()
        self.sent += self.copies
        self.copies = []

    def step(self):
        depth = len(self.stages)
        index = self.done
        self.done += 1
        if index < depth:
            self.scatter_finish(index)
            if index + 1 < depth:
                self.scatter_start(index + 1)
                return
            self.gather_own()
            self.gather_start(depth - 1)
            return
        self.gather_finish()
        if index + 1 < 2 * depth:
            self.gather_start(2 * depth - 2 - index)

    def pending(self):
        return self.done < 2 * len(self.stages)

    def drain(self):
        for made in self.sent:
            made.wait_send()


def reduction_rows(rows, devices):
    return -(-rows // (devices * ROW_TILE)) * ROW_TILE * devices


def reduction_scratch(stages, rows):
    shapes = [
        pltpu.VMEM((rows, LANES), jnp.float32),
        pltpu.VMEM((rows, LANES), jnp.bfloat16),
        pltpu.VMEM((rows, LANES), jnp.bfloat16),
    ]
    length, count = rows, 0
    for _, size, _ in stages:
        length //= size
        count += 2 * (size - 1)
        shapes.append(pltpu.VMEM((size - 1, length, LANES), jnp.bfloat16))
    return shapes + [pltpu.SemaphoreType.DMA((count,)), pltpu.SemaphoreType.DMA((count,))]


def greet(stages):
    barrier = pltpu.get_barrier_semaphore()
    count = 0
    for axis, size, stride in stages:
        for step in range(1, size):
            _, device = partner(axis, size, stride, step)
            pl.semaphore_signal(barrier, inc=1, device_id=device, device_id_type=pl.DeviceIdType.MESH)
            count += 1
    return count


def moved_planes(planes, row_tap, col_tap, row_count, col_count):
    offset = (row_tap - 1) * col_count + col_tap - 1
    if not offset:
        return planes
    total = planes.shape[1]
    lane = lax.broadcasted_iota(jnp.int32, (1, total), 1)
    col_at = lane % col_count + (col_tap - 1)
    row_at = lane // col_count % row_count + (row_tap - 1)
    inside = (row_at >= 0) & (row_at < row_count) & (col_at >= 0) & (col_at < col_count)
    keep = jnp.where(inside, 1.0, 0.0).astype(jnp.bfloat16)
    return pltpu.roll(planes, -offset % total, 1) * keep


def plane_taps():
    return [(row_tap, col_tap) for row_tap in range(3) for col_tap in range(3)]


def tap_rows(depth_tap, row_tap, col_tap, chans):
    tap = (depth_tap * 3 + row_tap) * 3 + col_tap
    return slice(tap * chans, (tap + 1) * chans)


def fill_inner(patches, planes, row_count, col_count):
    chans, span = planes.shape
    cells = row_count * col_count
    for taps in plane_taps():
        moved = moved_planes(planes, *taps, row_count, col_count)
        patches[tap_rows(0, *taps, chans), cells:] = moved[:, : span - cells]
        patches[tap_rows(1, *taps, chans)] = moved
        patches[tap_rows(2, *taps, chans), : span - cells] = moved[:, cells:]


def fill_outer(patches, edges, low, high, row_count, col_count):
    chans, cells = edges.shape[1:]
    span = patches.shape[1]
    first = (edges[0].astype(jnp.float32) * low).astype(jnp.bfloat16)
    last = (edges[1].astype(jnp.float32) * high).astype(jnp.bfloat16)
    planes = jnp.concatenate([first, last], axis=1)
    for taps in plane_taps():
        moved = moved_planes(planes, *taps, row_count, col_count)
        patches[tap_rows(0, *taps, chans), :cells] = moved[:, :cells]
        patches[tap_rows(2, *taps, chans), span - cells :] = moved[:, cells:]


def gelu_bend(values):
    return jnp.tanh(0.7978845608028654 * values * (1.0 + 0.044715 * values * values))


def gelu_slope(values, bend):
    outer = 0.7978845608028654 * (1.0 + 0.134145 * values * values)
    return 0.5 * (1.0 + bend) + 0.5 * values * (1.0 - bend * bend) * outer


def contract(left, right, left_dim, right_dim):
    return lax.dot_general(
        left, right, (((left_dim,), (right_dim,)), ((), ())), preferred_element_type=jnp.float32
    )


def pool_cells(values, row_count, col_count):
    cells = row_count * col_count
    pairs = [
        values[:, 2 * d * cells : (2 * d + 1) * cells] + values[:, (2 * d + 1) * cells : (2 * d + 2) * cells]
        for d in range(values.shape[1] // (2 * cells))
    ]
    paired = jnp.concatenate(pairs, axis=1)
    span = paired.shape[1]
    paired = paired + pltpu.roll(paired, span - 1, 1)
    paired = paired + pltpu.roll(paired, span - col_count, 1)
    small = cells // 4
    target = lax.broadcasted_iota(jnp.int32, (span, span // 4), 1)
    cell = target % small
    corner = (
        target // small * cells
        + cell // (col_count // 2) * (2 * col_count)
        + cell % (col_count // 2) * 2
    )
    here = lax.broadcasted_iota(jnp.int32, (span, span // 4), 0)
    picks = jnp.where(here == corner, 1.0, 0.0).astype(jnp.bfloat16)
    return contract((paired * 0.125).astype(jnp.bfloat16), picks, 1, 0).astype(jnp.bfloat16)


def spread_cells(values, row_count, col_count):
    cells = row_count * col_count
    chans, small_span = values.shape
    span = small_span * 8
    cell = lax.broadcasted_iota(jnp.int32, (small_span, span), 1)
    source = (
        cell // (2 * cells) * (cells // 4)
        + cell % cells // (2 * col_count) * (col_count // 2)
        + cell % col_count // 2
    )
    here = lax.broadcasted_iota(jnp.int32, (small_span, span), 0)
    copies = jnp.where(here == source, 1.0, 0.0).astype(jnp.bfloat16)
    high = values.astype(jnp.bfloat16)
    rest = values - high.astype(jnp.float32)
    middle = rest.astype(jnp.bfloat16)
    low = (rest - middle.astype(jnp.float32)).astype(jnp.bfloat16)
    wide = contract(jnp.concatenate([high, middle, low], axis=0), copies, 1, 0)
    return wide[:chans] + wide[chans : 2 * chans] + wide[2 * chans :]


def merged_planes(planes):
    wide = planes.astype(jnp.float32)
    parts = [wide[:, d, :] for d in range(planes.shape[1])]
    return jnp.concatenate(parts, axis=1).astype(planes.dtype)


def finish_kernel(scale, grad_in_ref, mid_ref, deep_ref, grad_in_out, mid_out, deep_out):
    half = mid_ref.shape[0]
    cells = grad_in_out.shape[2]
    packed = mid_ref[...].astype(jnp.float32) * scale
    mid_out[:half] = packed[:, : mid_out.shape[1]]
    mid_out[half:] = packed[:, mid_out.shape[1] :]
    deep_out[...] = deep_ref[...].astype(jnp.float32) * scale
    grad_in = grad_in_ref[...]
    planes = [grad_in[:, d * cells : (d + 1) * cells] for d in range(grad_in_out.shape[1])]
    grad_in_out[...] = jnp.stack(planes, axis=1).astype(jnp.bfloat16)


def block_kernel(plans, layout, *refs):
    refs = list(refs)

    def take(count):
        taken = refs[:count]
        del refs[:count]
        return taken

    inputs = take(4)
    grad_in_ref, mid_out, deep_out = take(3)
    mid_patches, deep_patches, deep_back, mid_back, mid_flip, deep_flip, mid_turned, deep_turned = take(8)
    held = take(4)
    load_sem, store_sem, grad_held = take(3)
    edges = [take(2) for _ in range(4)]
    edge_send, edge_recv = take(2)
    works = []
    for stages in plans:
        total, outgoing, gathered = take(3)
        landing = take(len(stages))
        works.append(Reduction(stages, total, outgoing, gathered, landing, take(2)))
    first, second, third = works
    loads = [pltpu.make_async_copy(*pair, load_sem.at[at]) for at, pair in enumerate(zip(inputs, held))]
    for load in loads:
        load.start()
    source_ref, cot_ref, mid_ref, deep_ref = held
    row_count, col_count = layout
    cells = row_count * col_count
    small = cells // 4
    chans1 = source_ref.shape[0]
    chans2, chans3 = deep_ref.shape[0] // 27, deep_ref.shape[1]
    dp, space = lax.axis_index("dp"), lax.axis_index("space")
    slabs = lax.axis_size("space")
    low = jnp.where(space > 0, 1.0, 0.0)
    high = jnp.where(space < slabs - 1, 1.0, 0.0)

    def swap_start(index, planes, cells_here):
        leaving, arriving = edges[index]
        if planes is not None:
            leaving[0] = planes[:, :cells_here]
            leaving[1] = planes[:, planes.shape[1] - cells_here :]
        made = []
        for side, other in ((0, lax.rem(space + slabs - 1, slabs)), (1, lax.rem(space + 1, slabs))):
            made.append(
                pltpu.make_async_remote_copy(
                    src_ref=leaving.at[side],
                    dst_ref=arriving.at[1 - side],
                    send_sem=edge_send.at[2 * index + side],
                    recv_sem=edge_recv.at[2 * index + side],
                    device_id=(dp, other),
                    device_id_type=pl.DeviceIdType.MESH,
                )
            )
            made[-1].start()
        return made

    def swap_finish(index, made, patches, row_count, col_count):
        for one in made:
            one.wait_recv()
        fill_outer(patches, edges[index][1], low, high, row_count, col_count)

    greeted = greet(plans[2])
    loads[0].wait()
    source = merged_planes(source_ref[...])
    edges[0][0][0] = source[:, :cells]
    edges[0][0][1] = source[:, source.shape[1] - cells :]
    pl.semaphore_wait(pltpu.get_barrier_semaphore(), greeted)
    swap0 = swap_start(0, None, cells)
    deep_rows = deep_ref.shape[0]
    cut = deep_rows // 2
    half = mid_out.shape[0]
    for work, used in ((first, cut), (second, deep_rows - cut), (third, half)):
        spare = work.total.shape[0] - used
        if spare:
            work.total[used:] = jnp.zeros((spare, LANES), jnp.float32)
    fill_inner(mid_patches, source, row_count, col_count)
    loads[2].wait()
    mid_turned[...] = mid_ref[...].T
    swap_finish(0, swap0, mid_patches, row_count, col_count)
    mid_pre = contract(mid_turned[...], mid_patches[...], 1, 0)
    mid_bend = gelu_bend(mid_pre)
    pooled = pool_cells(0.5 * mid_pre * (1.0 + mid_bend), row_count, col_count)
    swap1 = swap_start(1, pooled, small)
    fill_inner(deep_patches, pooled, row_count // 2, col_count // 2)
    loads[3].wait()
    deep_turned[...] = deep_ref[...].T
    loads[1].wait()
    upstream = cot_ref[...].astype(jnp.float32).T
    mid_slope = gelu_slope(mid_pre, mid_bend)
    swap_finish(1, swap1, deep_patches, row_count // 2, col_count // 2)
    deep_pre = contract(deep_turned[...], deep_patches[...], 1, 0)
    deep_grad = (upstream * gelu_slope(deep_pre, gelu_bend(deep_pre))).astype(jnp.bfloat16)
    swap2 = swap_start(2, deep_grad, small)
    first.total[:cut] = contract(deep_patches[:cut], deep_grad, 1, 1)
    first.scatter_start(0)
    second.total[: deep_rows - cut] = contract(deep_patches[cut:], deep_grad, 1, 1)
    second.scatter_start(0)
    fill_inner(deep_back, deep_grad, row_count // 2, col_count // 2)
    for tap in range(27):
        deep_flip[:, tap * chans3 : (tap + 1) * chans3] = deep_ref[(26 - tap) * chans2 : (27 - tap) * chans2]
    swap_finish(2, swap2, deep_back, row_count // 2, col_count // 2)
    back = contract(deep_flip[...], deep_back[...], 1, 0)
    mid_grad = (spread_cells(back, row_count, col_count) * 0.125 * mid_slope).astype(jnp.bfloat16)
    swap3 = swap_start(3, mid_grad, cells)
    first.step()
    second.step()
    third.total[:half] = jnp.concatenate(
        [contract(mid_patches[:half], mid_grad, 1, 1), contract(mid_patches[half:], mid_grad, 1, 1)], axis=1
    )
    third.scatter_start(0)
    fill_inner(mid_back, mid_grad, row_count, col_count)
    first.step()
    second.step()
    for tap in range(27):
        mid_flip[:, tap * chans2 : (tap + 1) * chans2] = mid_ref[(26 - tap) * chans1 : (27 - tap) * chans1]
    swap_finish(3, swap3, mid_back, row_count, col_count)
    third.step()
    grad_held[...] = contract(mid_flip[...], mid_back[...], 1, 0)
    stores = [pltpu.make_async_copy(grad_held, grad_in_ref, store_sem.at[0])]
    stores[0].start()
    while any(work.pending() for work in works):
        for work in works:
            if work.pending():
                work.step()
    for source, target in (
        (first.gathered.at[:cut], deep_out.at[:cut]),
        (second.gathered.at[: deep_rows - cut], deep_out.at[cut:]),
        (third.gathered.at[:half], mid_out),
    ):
        stores.append(pltpu.make_async_copy(source, target, store_sem.at[len(stores)]))
        stores[-1].start()
    for one in stores:
        one.wait()
    for one in swap0 + swap1 + swap2 + swap3:
        one.wait_send()
    for work in works:
        work.drain()


def shards(activations, cotangent, weight_mid, weight_deep):
    samples, slabs = lax.axis_size("dp"), lax.axis_size("space")
    stages = group_stages(samples, slabs)
    turned = stages[:1] + stages[1:][::-1]
    plans = (stages, turned, joined_stages(stages))
    chans1, chans2, chans3 = weight_mid.shape[3], weight_mid.shape[4], weight_deep.shape[4]
    source = activations[0]
    upstream = jnp.transpose(cotangent[0], (1, 2, 0)).reshape(-1, chans3)
    mid_flat = weight_mid.reshape(-1, chans2)
    deep_flat = weight_deep.reshape(-1, chans3)
    cells, small = source.shape[1] * source.shape[2], upstream.shape[0]
    plane, small_plane = ROWS * COLS, ROWS * COLS // 4
    half_rows = reduction_rows(-(-deep_flat.shape[0] // 2), samples * slabs)
    mid_rows = reduction_rows(mid_flat.shape[0] // 2, samples * slabs)
    scratch = [
        pltpu.VMEM((27 * chans1, cells), jnp.bfloat16),
        pltpu.VMEM((27 * chans2, small), jnp.bfloat16),
        pltpu.VMEM((27 * chans3, small), jnp.bfloat16),
        pltpu.VMEM((27 * chans2, cells), jnp.bfloat16),
        pltpu.VMEM((chans1, 27 * chans2), jnp.bfloat16),
        pltpu.VMEM((chans2, 27 * chans3), jnp.bfloat16),
        pltpu.VMEM(mid_flat.shape[::-1], jnp.bfloat16),
        pltpu.VMEM(deep_flat.shape[::-1], jnp.bfloat16),
        *(pltpu.VMEM(one.shape, jnp.bfloat16) for one in (source, upstream, mid_flat, deep_flat)),
        pltpu.SemaphoreType.DMA((4,)),
        pltpu.SemaphoreType.DMA((4,)),
        pltpu.VMEM((chans1, cells), jnp.float32),
    ]
    for chans, width in ((chans1, plane), (chans2, small_plane), (chans3, small_plane), (chans2, plane)):
        scratch += [pltpu.VMEM((2, chans, width), jnp.bfloat16)] * 2
    scratch += [pltpu.SemaphoreType.DMA((8,)), pltpu.SemaphoreType.DMA((8,))]
    for plan, rows in zip(plans, (half_rows, half_rows, mid_rows)):
        scratch += reduction_scratch(plan, rows)
    grad_in, mid_sum, deep_sum = pl.pallas_call(
        functools.partial(block_kernel, plans, (ROWS, COLS)),
        out_shape=[
            jax.ShapeDtypeStruct((chans1, cells), jnp.float32),
            jax.ShapeDtypeStruct((mid_flat.shape[0] // 2, LANES), jnp.bfloat16),
            jax.ShapeDtypeStruct(deep_flat.shape, jnp.bfloat16),
        ],
        in_specs=[pl.BlockSpec(memory_space=pltpu.HBM)] * 4,
        out_specs=[pl.BlockSpec(memory_space=pltpu.HBM)] * 3,
        scratch_shapes=scratch,
        compiler_params=pltpu.CompilerParams(
            collective_id=0, has_side_effects=True, vmem_limit_bytes=56 * 1024 * 1024
        ),
    )(source, upstream, mid_flat, deep_flat)
    grad_in, mid_sum, deep_sum = pl.pallas_call(
        functools.partial(finish_kernel, 1.0 / samples),
        out_shape=[
            jax.ShapeDtypeStruct(source.shape, jnp.bfloat16),
            jax.ShapeDtypeStruct(mid_flat.shape, jnp.float32),
            jax.ShapeDtypeStruct(deep_flat.shape, jnp.float32),
        ],
        in_specs=[pl.BlockSpec(memory_space=pltpu.VMEM)] * 3,
        out_specs=[pl.BlockSpec(memory_space=pltpu.VMEM)] * 3,
        compiler_params=pltpu.CompilerParams(vmem_limit_bytes=56 * 1024 * 1024),
    )(grad_in, mid_sum, deep_sum)
    return (
        grad_in.reshape(activations.shape),
        mid_sum.reshape(weight_mid.shape),
        deep_sum.reshape(weight_deep.shape),
    )


def solution(mesh):
    in_specs = (P("dp", None, "space", None), P("dp", None, "space", None), P(), P())
    out_specs = (P("dp", None, "space", None), P(), P())
    return jax.shard_map(shards, mesh=mesh, in_specs=in_specs, out_specs=out_specs, check_vma=False)
```
